32 devices in a mesh: wide: 8 (over z, y), narrow: 4 (over x, core).
Axes of the slice: x: 2, y: 2, z: 4, core: 2. Of those that a mesh axis runs over, the one named last changes fastest.
Arguments:
- trace_parts: float32 [16384, 384], P(('wide', 'narrow')), may hold values from -6 to 6
- node_slab: int32 [16384, 1], P(('wide', 'narrow')), may hold values from 0 to 7; in each aligned block of 512 rows (0 to 511, 512 to 1023, ...) at most 160 rows name the same one
- node_local: int32 [16384], P(('wide', 'narrow')), may hold values from 0 to 255
- solid_fraction: float32 [4, 2048], P('narrow', 'wide'), may hold values from 0.3 to 0.7
- influence: bfloat16 [4, 2048, 4, 2048], P(None, 'wide', 'narrow'), may hold values from -0.0625 to 0.0625
Outputs:
- boundary_potential: float32 [4, 2048, 384], P('narrow', 'wide')
- dirichlet: float32 [16384, 384], P(('wide', 'narrow'))
The draws below stay inside these ranges and needn't reach their ends.
Inputs may be any that keep to these rules, and one draw needn't show every extreme that they name: `node_slab`: in the slots of one partition at most 160 name one target slab; some partition reaches 160.
All inputs are finite; a program needn't handle non-finite values.
Results may differ from the reference program's by a relative error of at most 0.0026.
Values may be sent and summed in bfloat16 or wider, within the bound.
No kernel may reach another device: no remote copies, remote signals or barrier semaphores. Data moves between devices by JAX's collectives and lax.ppermute only.
A program may use at most 128 MiB of HBM per device.

```python
import math
import jax
import jax.numpy as jnp
import numpy as np
from jax import lax

NODE_DEV = 256
IMAGES = 384
SLOT_DEV = 512
CAP = 160
WIDE_NODES = 2048
NODES = 8192
SLOTS = 16384
N_WIDE = 8
N_NARROW = 4


def set_ends(entries, stream_key, least, high):
    shape = entries.shape
    index_at = [jax.random.randint(jax.random.fold_in(stream_key, axis), (), 0, shape[axis]) for axis in range(len(shape))]
    entries = entries.at[tuple(index_at)].set(least)
    longest = shape.index(max(shape))
    index_at[longest] = (index_at[longest] + 1) % shape[longest]
    return entries.at[tuple(index_at)].set(high)


def shard_levels(key, shape, shards, least, largest):
    def one(dim, blocks):
        steps = jax.random.uniform(jax.random.fold_in(jax.random.fold_in(key, 6), dim), (blocks,), jnp.float32, least / len(shards), largest / len(shards))
        return jnp.repeat(jnp.exp(steps), shape[dim] // blocks).reshape((-1,) + (1,) * (len(shape) - dim - 1))

    level = one(*shards[0])
    for cut in shards[1:]:
        level = level * one(*cut)
    return level


def routed_block(stream_key, own, number, rows, count, top, most, slope):
    sequence = jax.random.permutation(stream_key, count)
    heavy_load, usual = load_shares(count, rows * top, most, slope, True), load_shares(count, rows * top, most, slope, False)
    places = jnp.arange(count)

    def named(tallies, rotation):
        used = int((tallies > 0).sum())
        fixed = max(1, used // 4)
        shifted = fixed + (places - fixed + rotation * (used - fixed)) % max(1, count - fixed)
        return jnp.zeros((count,), jnp.int32).at[sequence[jnp.where(places < fixed, places, shifted)]].set(jnp.asarray(tallies, jnp.int32))

    tallies = jnp.where(number % 4 == 0, named(heavy_load, number // 4), named(usual, number - number // 4 - 1))
    mixed = jax.random.permutation(jax.random.fold_in(own, 3), count)
    giver, receiver = mixed[0:count // 2 * 2:2], mixed[1:count // 2 * 2:2]
    room = jnp.minimum(tallies[giver] - 1, most - tallies[receiver]) // 2
    room = jnp.where((giver == sequence[0]) | (receiver == sequence[0]) | (tallies[receiver] == 0), 0, jnp.maximum(room, 0))
    shifted = jax.random.randint(jax.random.fold_in(own, 4), (count // 2,), 0, 1 << 20) % (room + 1)
    tallies = tallies.at[giver].add(-shifted).at[receiver].add(shifted)
    items = jnp.searchsorted(jnp.cumsum(tallies), jnp.arange(rows * top), side="right").astype(jnp.int32)
    table = items.reshape(top, rows).T
    table = table[jax.random.permutation(jax.random.fold_in(own, 1), rows)]
    rotation = jax.random.randint(jax.random.fold_in(own, 2), (rows, 1), 0, top)
    return jnp.take_along_axis(table, (jnp.arange(top)[None, :] + rotation) % top, axis=1)


def load_shares(count, total, bound, skew, full):
    portions = [(1 << 20) // math.isqrt(standing ** skew) + 1 for standing in range(1, count + 1)]
    largest = bound if full else min(bound, max(-(-total // count), total * portions[0] // sum(portions)))
    least = 1 if total - largest >= count - 1 else 0
    counts, rest = [largest] + [least] * (count - 1), total - largest - least * (count - 1)
    while rest > 0:
        free = [i for i in range(1, count) if counts[i] < largest] or [i for i in range(1, count) if counts[i] < bound]
        mass, remaining = sum([portions[i] for i in free]), rest
        for i in free:
            addition = min(bound - counts[i], max(1, remaining * portions[i] // mass), rest)
            counts[i] = counts[i] + addition
            rest = rest - addition
    return np.array(counts)


def gaussian(key, extent, spread, bound, cuts=(), kind=jnp.bfloat16):
    level = shard_levels(key, extent, cuts, -0.22, 0.18) if cuts else 1.0
    array = jax.random.normal(key, extent, jnp.float32) * spread * level
    return jnp.minimum(jnp.maximum(array, -bound), bound).astype(kind)


def setup_inputs(seed: int = 0) -> dict:
    seeds = jax.random.split(jax.random.key(seed), 6)
    trace_parts = gaussian(seeds[0], (SLOTS, IMAGES), 1.0, 6.0, ((0, 32),), jnp.float32)
    node_slab_keys = jax.random.split(jax.random.fold_in(seeds[1], 1), SLOTS // SLOT_DEV)
    node_slab_turns = jax.random.permutation(jax.random.fold_in(seeds[1], 3), SLOTS // SLOT_DEV)
    node_slab = jax.vmap(lambda own, number: routed_block(jax.random.fold_in(seeds[1], 2), own, number, SLOT_DEV, N_WIDE, 1, CAP, 2))(node_slab_keys, node_slab_turns).reshape((SLOTS, 1))
    node_local = set_ends(jax.random.randint(seeds[2], (SLOTS,), 0, NODE_DEV), jax.random.fold_in(seeds[2], 1), 0, NODE_DEV - 1).astype(jnp.int32)
    solid_fraction = jnp.clip(0.3 + 0.39999998 * jax.random.uniform(seeds[3], (N_NARROW, WIDE_NODES), jnp.float32) ** shard_levels(seeds[3], (N_NARROW, WIDE_NODES), ((0, 4), (1, 8)), -0.2, 0.2), 0.3, 0.7)
    influence = gaussian(seeds[4], (N_NARROW, WIDE_NODES, N_NARROW, WIDE_NODES), NODES ** -0.5, 0.0625, ((1, 8), (2, 4)))
    return {"trace_parts": trace_parts, "node_slab": node_slab, "node_local": node_local, "solid_fraction": solid_fraction, "influence": influence}


def reference(trace_parts, node_slab, node_local, solid_fraction, influence):
    device_of = jnp.arange(SLOTS, dtype=jnp.int32) // SLOT_DEV
    narrow_of = device_of % N_NARROW
    flat_node = (narrow_of * WIDE_NODES + node_slab[:, 0] * NODE_DEV + node_local).astype(jnp.int32)
    first_trace = jnp.zeros((NODES, IMAGES), jnp.float32).at[flat_node].add(trace_parts)
    trace_round = first_trace.astype(jnp.bfloat16)
    matrix_rows = influence.reshape(N_NARROW, WIDE_NODES, NODES)

    def one_block(block_rows):
        return jnp.dot(block_rows, trace_round, preferred_element_type=jnp.float32)

    layer = lax.map(one_block, matrix_rows).reshape(NODES, IMAGES)
    boundary_flat = layer + (solid_fraction.reshape(NODES)[:, None] - 1.0) * first_trace
    dirichlet = boundary_flat[flat_node]
    return (boundary_flat.reshape(N_NARROW, WIDE_NODES, IMAGES), dirichlet)
```

```python
import jax
import jax.numpy as jnp
from jax import lax
from jax.experimental import pallas as pl
from jax.experimental.pallas import tpu as pltpu
from jax.sharding import PartitionSpec as P

TRACE_SCALE = 2.0**13
RESULT_SCALE = 2.0
VMEM = 56 * 2**20
GROUP = 8


def exchange(block, axis, offset):
    count = lax.axis_size(axis)
    return lax.ppermute(block, axis, [(i, i ^ offset) for i in range(count)])


def gather_blocks(block):
    count = lax.axis_size("wide")
    held = {0: block}
    for offset in (2, 4, 6):
        if offset < count:
            held[offset] = exchange(block, "wide", offset)
    step = 1
    while step < count:
        if step not in held:
            for offset in sorted(held):
                held[offset ^ step] = exchange(held[offset], "wide", step)
        step *= 2
    return held


def halves(values):
    high = lax.reduce_precision(values, 8, 7)
    return jnp.concatenate([high, values - high], axis=-1).astype(jnp.bfloat16)


def scatter_tile(ids_ref, blocks, first_node, node_dev):
    slots = blocks[0].shape[0]
    node = first_node + lax.broadcasted_iota(jnp.int32, (node_dev, slots), 0)
    total = None
    for row, block in enumerate(blocks):
        pick = jnp.where(ids_ref[row : row + 1, :] == node, 1.0, 0.0).astype(jnp.bfloat16)
        term = jnp.dot(pick, block[...], preferred_element_type=jnp.float32)
        total = term if total is None else total + term
    images = total.shape[1] // 2
    return total[:, :images] + total[:, images:]


def scatter(ids, blocks, before, nodes, node_dev):
    slots, images = blocks[0].shape[0], blocks[0].shape[1] // 2

    def body(*refs):
        ids_ref, rest = refs[0], refs[1:]
        out = rest[-1]
        total = scatter_tile(ids_ref, rest[: len(blocks)], pl.program_id(0) * node_dev, node_dev)
        if before is not None:
            total = total + rest[len(blocks)][...]
        out[...] = total

    tile = pl.BlockSpec((node_dev, images), lambda s: (s, 0))
    whole = pl.BlockSpec((slots, 2 * images), lambda s: (0, 0))
    more = [] if before is None else [before]
    return pl.pallas_call(
        body,
        grid=(nodes // node_dev,),
        in_specs=[pl.BlockSpec(ids.shape, lambda s: (0, 0))] + [whole] * len(blocks) + [tile] * len(more),
        out_specs=tile,
        out_shape=jax.ShapeDtypeStruct((nodes, images), jnp.float32),
        compiler_params=pltpu.CompilerParams(vmem_limit_bytes=VMEM),
        name="scatter_traces",
    )(ids, *blocks, *more)


def scatter_and_layer(place, ids, blocks, before, matrix, nodes, node_dev):
    slots, images = blocks[0].shape[0], blocks[0].shape[1] // 2
    rows = matrix.shape[0]

    def body(place_ref, ids_ref, *rest):
        before_ref, matrix_ref, layer_ref, own_ref = rest[len(blocks) :]
        step = pl.program_id(0)
        total = scatter_tile(ids_ref, rest[: len(blocks)], step * node_dev, node_dev)
        total = (total + before_ref[...]) * (1.0 / TRACE_SCALE)

        @pl.when(step == place_ref[0])
        def _():
            own_ref[...] = total

        term = jnp.dot(matrix_ref[...], total.astype(jnp.bfloat16), preferred_element_type=jnp.float32)

        @pl.when(step == 0)
        def _():
            layer_ref[...] = term

        @pl.when(step != 0)
        def _():
            layer_ref[...] += term

    whole = pl.BlockSpec((slots, 2 * images), lambda s, p: (0, 0))
    return pl.pallas_call(
        body,
        grid_spec=pltpu.PrefetchScalarGridSpec(
            num_scalar_prefetch=1,
            grid=(nodes // node_dev,),
            in_specs=[pl.BlockSpec(ids.shape, lambda s, p: (0, 0))]
            + [whole] * len(blocks)
            + [
                pl.BlockSpec((node_dev, images), lambda s, p: (s, 0)),
                pl.BlockSpec((rows, node_dev), lambda s, p: (0, s)),
            ],
            out_specs=[
                pl.BlockSpec((rows, images), lambda s, p: (0, 0)),
                pl.BlockSpec((node_dev, images), lambda s, p: (0, 0)),
            ],
        ),
        out_shape=[
            jax.ShapeDtypeStruct((rows, images), jnp.float32),
            jax.ShapeDtypeStruct((node_dev, images), jnp.float32),
        ],
        compiler_params=pltpu.CompilerParams(vmem_limit_bytes=VMEM),
        name="scatter_and_layer",
    )(place, ids, *blocks, before, matrix)


def read_back(place, ids, table, count, node_dev):
    slots, images = ids.shape[0], table.shape[1] // 2

    def body(place_ref, ids_ref, table_ref, out_ref):
        total = jnp.zeros((slots, 2 * images), jnp.float32)
        lane = lax.broadcasted_iota(jnp.int32, (slots, node_dev), 1)
        for k in range(count):
            node = (place_ref[0] ^ k) * node_dev + lane
            pick = jnp.where(ids_ref[...] == node, 1.0, 0.0).astype(jnp.bfloat16)
            total += jnp.dot(
                pick, table_ref[k * node_dev : (k + 1) * node_dev, :], preferred_element_type=jnp.float32
            )
        out_ref[...] = (total[:, :images] + total[:, images:]) * (1.0 / RESULT_SCALE)

    return pl.pallas_call(
        body,
        in_specs=[
            pl.BlockSpec(memory_space=pltpu.SMEM),
            pl.BlockSpec(memory_space=pltpu.VMEM),
            pl.BlockSpec(memory_space=pltpu.VMEM),
        ],
        out_shape=jax.ShapeDtypeStruct((slots, images), jnp.float32),
        compiler_params=pltpu.CompilerParams(vmem_limit_bytes=VMEM),
        name="read_back",
    )(place, ids, table)


def on_device(trace_parts, node_slab, node_local, solid_fraction, influence):
    node_dev = solid_fraction.shape[1]
    images = trace_parts.shape[1]
    wide_count = lax.axis_size("wide")
    narrow_count = lax.axis_size("narrow")
    nodes = wide_count * node_dev
    me = lax.axis_index("wide")
    place = me.astype(jnp.int32).reshape(1)

    ids = node_slab[:, 0] * node_dev + node_local
    ids_all = lax.all_gather(ids, "wide", axis=0, tiled=False)
    order = sorted(range(wide_count), key=lambda k: (k & 1) + 2 * (k >> 2) if wide_count == 8 else k)
    ids_order = ids_all[me ^ jnp.array(order, jnp.int32)]

    sent = (trace_parts * TRACE_SCALE).astype(jnp.float16)
    held = gather_blocks(sent)
    blocks = [halves(held[k].astype(jnp.float32)) for k in order]

    last = min(GROUP, wide_count) // 2
    before = None
    done = 0
    while done < wide_count - last:
        size = min(GROUP, wide_count - last - done)
        before = scatter(ids_order[done : done + size], blocks[done : done + size], before, nodes, node_dev)
        done += size
    matrix = influence.reshape(narrow_count * node_dev, nodes)
    partial, own_trace = scatter_and_layer(
        place, ids_order[done:], blocks[done:], before, matrix, nodes, node_dev
    )

    parts = partial.reshape(narrow_count, node_dev, images)
    column = lax.axis_index("narrow")
    layer = lax.dynamic_index_in_dim(parts, column, 0, keepdims=False)
    for k in range(1, narrow_count):
        share = lax.dynamic_index_in_dim(parts, column ^ k, 0, keepdims=False)
        share = (share * RESULT_SCALE).astype(jnp.float16)
        layer = layer + exchange(share, "narrow", k).astype(jnp.float32) * (1.0 / RESULT_SCALE)
    potential = layer + (solid_fraction[0, :, None] - 1.0) * own_trace

    spread = gather_blocks((potential * RESULT_SCALE).astype(jnp.float16))
    table = halves(jnp.concatenate([spread[k] for k in range(wide_count)], axis=0).astype(jnp.float32))
    dirichlet = read_back(place, ids.reshape(-1, 1), table, wide_count, node_dev)
    return (potential[None], dirichlet)


def solution(mesh):
    placed = (
        P(("wide", "narrow"), None),
        P(("wide", "narrow"), None),
        P(("wide", "narrow")),
        P("narrow", "wide"),
        P(None, "wide", "narrow", None),
    )
    return jax.shard_map(
        on_device,
        mesh=mesh,
        in_specs=placed,
        out_specs=(P("narrow", "wide", None), P(("wide", "narrow"), None)),
        check_vma=False,
    )
```

```python
import jax
import jax.numpy as jnp
from jax import lax
from jax.experimental import pallas as pl
from jax.experimental.pallas import tpu as pltpu
from jax.sharding import PartitionSpec as P

TRACE_SCALE = 2.0**13
RESULT_SCALE = 2.0
MIB = 2**20
ROWS = 16


def exchange(block, axis, offset):
    count = lax.axis_size(axis)
    return lax.ppermute(block, axis, [(i, i ^ offset) for i in range(count)])


def after(value, *others):
    return lax.optimization_barrier((value, *others))[0]


def gather_blocks(block, early, late):
    count = lax.axis_size("wide")
    held = {0: block}
    held[4] = exchange(block, "wide", 4)
    held[2] = exchange(block, "wide", 2)
    held[1] = exchange(block, "wide", 1)
    held[6] = exchange(block, "wide", 6)
    held[3] = exchange(held[2], "wide", 1)
    done = early(held)
    held[4] = after(held[4], done)
    held[5] = exchange(held[4], "wide", 1)
    held[7] = exchange(held[6], "wide", 1)
    done = late(held, done)
    held[5], held[7], done = lax.optimization_barrier((held[5], held[7], done))
    step = 8
    while step < count:
        for offset in sorted(held):
            held[offset ^ step] = exchange(held[offset], "wide", step)
        step *= 2
    return held, done


def with_ids(values, slab, local):
    slots, images = values.shape
    per = -(-slots // images)
    extra = -(-2 * per // ROWS) * ROWS
    total = jnp.pad(values, ((0, extra), (0, 0)))
    for n, part in enumerate((slab, local)):
        for r in range(per):
            piece = part.reshape(1, slots)[:, r * images : (r + 1) * images].astype(values.dtype)
            row = n * per + r
            total = total + jnp.pad(piece, ((slots + row, extra - row - 1), (0, images - piece.shape[1])))
    return total.astype(jnp.float16)


def ids_of(block, slots, node_dev):
    images = block.shape[1]
    per = -(-slots // images)

    def line(first):
        pieces = [
            block[slots + first + r : slots + first + r + 1, : min(images, slots - r * images)] for r in range(per)
        ]
        return pieces[0] if per == 1 else jnp.concatenate(pieces, axis=1)

    return (line(0) * node_dev + line(per)).astype(jnp.int32)


def store_halves(values, out, first):
    rows, images = values.shape
    high = values.astype(jnp.bfloat16)
    out[first : first + rows, :images] = high
    out[first : first + rows, images:] = (values - high.astype(jnp.float32)).astype(jnp.bfloat16)


def scatter_tile(blocks, both, slots, first_node, tile, node_dev):
    @pl.when(first_node == 0)
    def _():
        for k, block in enumerate(blocks):
            store_halves(block[:slots, :], both, k * slots)

    node = first_node + lax.broadcasted_iota(jnp.int32, (tile, slots), 0)
    picks = [
        jnp.where(ids_of(block, slots, node_dev) == node, 1.0, 0.0).astype(jnp.bfloat16) for block in blocks
    ]
    total = jnp.dot(jnp.concatenate(picks, axis=1), both[...], preferred_element_type=jnp.float32)
    images = total.shape[1] // 2
    return total[:, :images] + total[:, images:]


def cost_of(blocks, slots, nodes, extra=0):
    images = blocks[0].shape[1]
    flops = 4 * len(blocks) * slots * nodes * images + extra
    return pl.CostEstimate(flops=flops, bytes_accessed=8 * nodes * images, transcendentals=0)


def scatter(blocks, slots, before, nodes, node_dev):
    images = blocks[0].shape[1]
    tile = 2 * node_dev

    def body(*refs):
        held, out, both = refs[: len(blocks)], refs[-2], refs[-1]
        total = scatter_tile(held, both, slots, pl.program_id(0) * tile, tile, node_dev)
        if before is not None:
            total = total + refs[len(blocks)][...]
        out[...] = total

    part = pl.BlockSpec((tile, images), lambda s: (s, 0))
    more = [] if before is None else [before]
    return pl.pallas_call(
        body,
        grid=(nodes // tile,),
        in_specs=[pl.BlockSpec(block.shape, lambda s: (0, 0)) for block in blocks] + [part] * len(more),
        out_specs=part,
        out_shape=jax.ShapeDtypeStruct((nodes, images), jnp.float32),
        scratch_shapes=[pltpu.VMEM((len(blocks) * slots, 2 * images), jnp.bfloat16)],
        compiler_params=pltpu.CompilerParams(vmem_limit_bytes=(8 + 4 * len(blocks)) * MIB),
        cost_estimate=cost_of(blocks, slots, nodes),
        name="scatter_traces",
    )(*blocks, *more)


def scatter_and_layer(place, blocks, slots, before, matrix, diagonal, nodes, node_dev, narrow_count):
    images = blocks[0].shape[1]
    tile = 2 * node_dev
    steps = nodes // tile

    def body(place_ref, *refs):
        held = refs[: len(blocks)]
        before_ref, matrix_ref, diagonal_ref = refs[len(blocks) : len(blocks) + 3]
        outs = refs[len(blocks) + 3 : -5]
        both, rounded, own, matrix_held, sem = refs[-5:]
        step = pl.program_id(0)
        fetch = pltpu.make_async_copy(matrix_ref, matrix_held, sem)

        @pl.when(step == 0)
        def _():
            fetch.start()

        total = scatter_tile(held, both, slots, step * tile, tile, node_dev)
        total = (total + before_ref[...]) * (1.0 / TRACE_SCALE)
        for half in range(2):
            @pl.when(2 * step + half == place_ref[0])
            def _():
                own[...] = total[half * node_dev : (half + 1) * node_dev, :]

        rounded[pl.ds(pl.multiple_of(step * tile, tile), tile), :] = total.astype(jnp.bfloat16)

        @pl.when(step == steps - 1)
        def _():
            fetch.wait()
            for k in range(narrow_count):
                first = pl.multiple_of((place_ref[1] ^ k) * node_dev, node_dev)
                layer = jnp.dot(
                    matrix_held[pl.ds(first, node_dev), :], rounded[...], preferred_element_type=jnp.float32
                )
                if k == 0:
                    layer = layer + diagonal_ref[...] * own[...]
                outs[k][...] = layer.astype(outs[k].dtype)

    one = pl.BlockSpec((node_dev, images), lambda s, p: (0, 0))
    limit = 12 + 4 * len(blocks) + (2 * matrix.size + 2 * nodes * images) // MIB
    return pl.pallas_call(
        body,
        grid_spec=pltpu.PrefetchScalarGridSpec(
            num_scalar_prefetch=1,
            grid=(steps,),
            in_specs=[pl.BlockSpec(block.shape, lambda s, p: (0, 0)) for block in blocks]
            + [
                pl.BlockSpec((tile, images), lambda s, p: (s, 0)),
                pl.BlockSpec(memory_space=pl.ANY),
                pl.BlockSpec((node_dev, 1), lambda s, p: (0, 0)),
            ],
            out_specs=[one] * narrow_count,
            scratch_shapes=[
                pltpu.VMEM((len(blocks) * slots, 2 * images), jnp.bfloat16),
                pltpu.VMEM((nodes, images), jnp.bfloat16),
                pltpu.VMEM((node_dev, images), jnp.float32),
                pltpu.VMEM(matrix.shape, matrix.dtype),
                pltpu.SemaphoreType.DMA,
            ],
        ),
        out_shape=[jax.ShapeDtypeStruct((node_dev, images), jnp.float32)]
        + [jax.ShapeDtypeStruct((node_dev, images), jnp.bfloat16)] * (narrow_count - 1),
        compiler_params=pltpu.CompilerParams(vmem_limit_bytes=limit * MIB),
        cost_estimate=cost_of(blocks, slots, nodes, 2 * matrix.shape[0] * nodes * images),
        name="scatter_and_layer",
    )(place, *blocks, before, matrix, diagonal)


def read_back(place, ids, blocks, keys, before):
    slots = ids.shape[0]
    node_dev, images = blocks[0].shape

    def body(place_ref, ids_ref, *refs):
        out, both = refs[-2:]
        lane = lax.broadcasted_iota(jnp.int32, (slots, node_dev), 1)
        picks = []
        for row, key in enumerate(keys):
            store_halves(refs[row][...], both, row * node_dev)
            node = (place_ref[0] ^ key) * node_dev + lane
            picks.append(jnp.where(ids_ref[...] == node, 1.0, 0.0).astype(jnp.bfloat16))
        total = jnp.dot(jnp.concatenate(picks, axis=1), both[...], preferred_element_type=jnp.float32)
        total = (total[:, :images] + total[:, images:]) * (1.0 / RESULT_SCALE)
        if before is not None:
            total = total + refs[len(blocks)][...]
        out[...] = total

    more = [] if before is None else [before]
    vmem = pl.BlockSpec(memory_space=pltpu.VMEM)
    return pl.pallas_call(
        body,
        in_specs=[pl.BlockSpec(memory_space=pltpu.SMEM)] + [vmem] * (1 + len(blocks) + len(more)),
        out_shape=jax.ShapeDtypeStruct((slots, images), jnp.float32),
        scratch_shapes=[pltpu.VMEM((len(blocks) * node_dev, 2 * images), jnp.bfloat16)],
        compiler_params=pltpu.CompilerParams(vmem_limit_bytes=(10 + 2 * len(blocks)) * MIB),
        cost_estimate=cost_of(blocks, node_dev, slots),
        name="read_back",
    )(place, ids, *blocks, *more)


def on_device(trace_parts, node_slab, node_local, solid_fraction, influence):
    node_dev = solid_fraction.shape[1]
    slots, images = trace_parts.shape
    wide_count = lax.axis_size("wide")
    narrow_count = lax.axis_size("narrow")
    nodes = wide_count * node_dev
    place = jnp.stack([lax.axis_index("wide"), lax.axis_index("narrow")]).astype(jnp.int32)
    ids = (node_slab[:, 0] * node_dev + node_local).reshape(-1, 1)
    diagonal = (solid_fraction - 1.0).reshape(-1, 1)
    first, second, last = (0, 1, 2), (3, 4, 6), (5, 7)
    others = [tuple(range(k, k + 4)) for k in range(8, wide_count, 4)]

    def add_up(held, keys, before):
        return scatter([held[k].astype(jnp.float32) for k in keys], slots, before, nodes, node_dev)

    sent = with_ids(trace_parts * TRACE_SCALE, node_slab, node_local)
    held, sums = gather_blocks(
        sent, lambda held: add_up(held, first, None), lambda held, sums: add_up(held, second, sums)
    )
    for keys in others:
        sums = add_up(held, keys, sums)
    matrix = influence.reshape(narrow_count * node_dev, nodes)
    potential, *shares = scatter_and_layer(
        place, [held[k].astype(jnp.float32) for k in last], slots, sums, matrix, diagonal, nodes, node_dev, narrow_count
    )
    for k, share in enumerate(shares, 1):
        potential = potential + exchange(share, "narrow", k).astype(jnp.float32)

    def look_up(held, keys, before):
        return read_back(place, ids, [held[k].astype(jnp.float32) for k in keys], keys, before)

    spread, dirichlet = gather_blocks(
        (potential * RESULT_SCALE).astype(jnp.float16),
        lambda held: look_up(held, first, None),
        lambda held, found: look_up(held, second, found),
    )
    for keys in others + [last]:
        dirichlet = look_up(spread, keys, dirichlet)
    return (potential[None], dirichlet)


def solution(mesh):
    placed = (
        P(("wide", "narrow"), None),
        P(("wide", "narrow"), None),
        P(("wide", "narrow")),
        P("narrow", "wide"),
        P(None, "wide", "narrow", None),
    )
    return jax.shard_map(
        on_device,
        mesh=mesh,
        in_specs=placed,
        out_specs=(P("narrow", "wide", None), P(("wide", "narrow"), None)),
        check_vma=False,
    )
```

```python
import jax
import jax.numpy as jnp
from jax import lax
from jax.experimental import pallas as pl
from jax.experimental.pallas import tpu as pltpu
from jax.sharding import PartitionSpec as P

TRACE_SCALE = 2.0**13
RESULT_SCALE = 2.0
MIB = 2**20
ROWS = 16
EXACT = 2048


def exchange(block, axis, offset):
    count = lax.axis_size(axis)
    return lax.ppermute(block, axis, [(i, i ^ offset) for i in range(count)])


def after(value, *others):
    return lax.optimization_barrier((value, *others))[0]


def gather_far(parts, split):
    whole, pieces = parts
    held = {0: [whole]}
    held[4] = [exchange(whole, "wide", 4)]
    held[2] = [exchange(whole, "wide", 2)]
    held[1] = [exchange(whole, "wide", 1)]
    if split:
        held[6] = [exchange(pieces[0], "wide", 6)]
        held[6].append(exchange(after(pieces[1], held[1][0]), "wide", 6))
    else:
        held[6] = [exchange(whole, "wide", 6)]
    return held


def id_parts(slab, local, nodes, node_dev):
    return [slab * node_dev + local] if nodes <= EXACT else [slab, local]


def with_ids(values, parts):
    slots, images = values.shape
    per = -(-slots // images)
    extra = -(-len(parts) * per // ROWS) * ROWS
    total = jnp.pad(values, ((extra, 0), (0, 0)))
    for n, part in enumerate(parts):
        for r in range(per):
            piece = part.reshape(1, slots)[:, r * images : (r + 1) * images].astype(values.dtype)
            row = n * per + r
            total = total + jnp.pad(piece, ((row, extra + slots - row - 1), (0, images - piece.shape[1])))
    return total.astype(jnp.float16)


def ids_of(tail, slots, nodes, node_dev):
    images = tail.shape[1]
    per = -(-slots // images)

    def line(first):
        pieces = [tail[first + r : first + r + 1, : min(images, slots - r * images)] for r in range(per)]
        return pieces[0] if per == 1 else jnp.concatenate(pieces, axis=1)

    return (line(0) if nodes <= EXACT else line(0) * node_dev + line(per)).astype(jnp.int32)


def store_halves(values, out, first):
    rows, images = values.shape
    high = values.astype(jnp.bfloat16)
    out[first : first + rows, :images] = high
    out[first : first + rows, images:] = (values - high.astype(jnp.float32)).astype(jnp.bfloat16)


class Rows:
    def __init__(self, data, tail, first, span):
        self.data, self.tail, self.first, self.span = data, tail, first, span
        self.count = span[1] - span[0]


def row_specs(rows):
    return [pl.BlockSpec(memory_space=pltpu.VMEM)] * (2 * len(rows))


def row_args(rows):
    return [array for part in rows for array in (part.data, part.tail)]


def scatter_tile(rows, refs, both, first_node, tile, slots, nodes, node_dev):
    @pl.when(first_node == 0)
    def _():
        done = 0
        for part, data in zip(rows, refs[::2]):
            store_halves(data[part.first : part.first + part.count, :], both, done)
            done += part.count

    picks = []
    for part, tail in zip(rows, refs[1::2]):
        node = first_node + lax.broadcasted_iota(jnp.int32, (tile, part.count), 0)
        ids = ids_of(tail, slots, nodes, node_dev)[:, part.span[0] : part.span[1]]
        picks.append(jnp.where(ids == node, 1.0, 0.0).astype(jnp.bfloat16))
    total = jnp.dot(jnp.concatenate(picks, axis=1), both[...], preferred_element_type=jnp.float32)
    images = total.shape[1] // 2
    return total[:, :images] + total[:, images:]


def scatter(rows, slots, before, nodes, node_dev):
    images = rows[0].data.shape[1]
    tile = 2 * node_dev
    depth = sum(part.count for part in rows)

    def body(*refs):
        out, both = refs[-2:]
        total = scatter_tile(rows, refs[: 2 * len(rows)], both, pl.program_id(0) * tile, tile, slots, nodes, node_dev)
        if before is not None:
            total = total + refs[2 * len(rows)][...]
        out[...] = total

    part = pl.BlockSpec((tile, images), lambda s: (s, 0))
    more = [] if before is None else [before]
    return pl.pallas_call(
        body,
        grid=(nodes // tile,),
        in_specs=row_specs(rows) + [part] * len(more),
        out_specs=part,
        out_shape=jax.ShapeDtypeStruct((nodes, images), jnp.float32),
        scratch_shapes=[pltpu.VMEM((depth, 2 * images), jnp.bfloat16)],
        compiler_params=pltpu.CompilerParams(vmem_limit_bytes=(8 + 2 * -(-depth // slots)) * MIB),
        cost_estimate=pl.CostEstimate(
            flops=4 * depth * nodes * images, bytes_accessed=8 * nodes * images, transcendentals=0
        ),
        name="scatter_traces",
    )(*row_args(rows), *more)


def row_block(place_ref, job, parts):
    offset, part = job
    return (place_ref[1] ^ offset) * parts + part


def scatter_and_layer(place, rows, slots, before, matrix, jobs, parts, nodes, node_dev):
    images = rows[0].data.shape[1]
    tile = 2 * node_dev
    steps = nodes // tile
    depth = sum(part.count for part in rows)
    count = len(jobs)
    height = node_dev // parts

    def body(place_ref, *refs):
        before_ref, matrix_ref = refs[2 * len(rows) : 2 * len(rows) + 2]
        rounded, own = refs[2 * len(rows) + 2 : 2 * len(rows) + 4]
        outs = refs[2 * len(rows) + 4 : -3]
        both, matrix_held, sems = refs[-3:]
        step = pl.program_id(0)
        fetches = []
        for n, job in enumerate(jobs):
            first = pl.multiple_of(row_block(place_ref, job, parts) * height, height)
            fetches.append(
                pltpu.make_async_copy(matrix_ref.at[pl.ds(first, height), :], matrix_held.at[n], sems.at[n])
            )

        @pl.when(step == 0)
        def _():
            for fetch in fetches:
                fetch.start()

        total = scatter_tile(rows, refs[: 2 * len(rows)], both, step * tile, tile, slots, nodes, node_dev)
        total = (total + before_ref[...]) * (1.0 / TRACE_SCALE)
        for half in range(2):
            @pl.when(2 * step + half == place_ref[0])
            def _():
                own[...] = total[half * node_dev : (half + 1) * node_dev, :]

        rounded[pl.ds(pl.multiple_of(step * tile, tile), tile), :] = total.astype(jnp.bfloat16)

        @pl.when(step == steps - 1)
        def _():
            for n, fetch in enumerate(fetches):
                fetch.wait()
                layer = jnp.dot(matrix_held[n], rounded[...], preferred_element_type=jnp.float32)
                outs[n][...] = layer.astype(outs[n].dtype)

    one = pl.BlockSpec((height, images), lambda s, p: (0, 0))
    limit = 10 + 2 * -(-depth // slots) + (2 * count * height * nodes + 4 * nodes * images) // MIB
    return pl.pallas_call(
        body,
        grid_spec=pltpu.PrefetchScalarGridSpec(
            num_scalar_prefetch=1,
            grid=(steps,),
            in_specs=row_specs(rows)
            + [pl.BlockSpec((tile, images), lambda s, p: (s, 0)), pl.BlockSpec(memory_space=pl.ANY)],
            out_specs=[
                pl.BlockSpec((nodes, images), lambda s, p: (0, 0)),
                pl.BlockSpec((node_dev, images), lambda s, p: (0, 0)),
            ]
            + [one] * count,
            scratch_shapes=[
                pltpu.VMEM((depth, 2 * images), jnp.bfloat16),
                pltpu.VMEM((count, height, nodes), matrix.dtype),
                pltpu.SemaphoreType.DMA((count,)),
            ],
        ),
        out_shape=[
            jax.ShapeDtypeStruct((nodes, images), jnp.bfloat16),
            jax.ShapeDtypeStruct((node_dev, images), jnp.float32),
        ]
        + [jax.ShapeDtypeStruct((height, images), jnp.bfloat16)] * count,
        compiler_params=pltpu.CompilerParams(vmem_limit_bytes=limit * MIB),
        cost_estimate=pl.CostEstimate(
            flops=4 * depth * nodes * images + 2 * count * height * nodes * images,
            bytes_accessed=8 * nodes * images,
            transcendentals=0,
        ),
        name="scatter_and_layer",
    )(place, *row_args(rows), before, matrix)


def layer_more(place, rounded, own, matrix, diagonal, jobs, parts):
    node_dev, images = own.shape
    nodes = rounded.shape[0]
    count = len(jobs)
    height = node_dev // parts

    def body(place_ref, rounded_ref, own_ref, diagonal_ref, *refs):
        for n, (offset, part) in enumerate(jobs):
            layer = jnp.dot(refs[n][...], rounded_ref[...], preferred_element_type=jnp.float32)
            if offset == 0:
                here = slice(part * height, (part + 1) * height)
                layer = layer + diagonal_ref[here, :] * own_ref[here, :]
            refs[count + n][...] = layer.astype(refs[count + n].dtype)

    def spec(array):
        return pl.BlockSpec(array.shape, lambda i, p: (0, 0))

    return pl.pallas_call(
        body,
        grid_spec=pltpu.PrefetchScalarGridSpec(
            num_scalar_prefetch=1,
            grid=(1,),
            in_specs=[spec(rounded), spec(own), spec(diagonal)]
            + [pl.BlockSpec((height, nodes), lambda i, p, job=job: (row_block(p, job, parts), 0)) for job in jobs],
            out_specs=[pl.BlockSpec((height, images), lambda i, p: (0, 0))] * count,
        ),
        out_shape=[
            jax.ShapeDtypeStruct((height, images), jnp.float32 if offset == 0 else jnp.bfloat16)
            for offset, _ in jobs
        ],
        compiler_params=pltpu.CompilerParams(
            vmem_limit_bytes=(8 + (4 * nodes * images + 4 * count * height * nodes) // MIB) * MIB
        ),
        cost_estimate=pl.CostEstimate(
            flops=2 * count * height * nodes * images, bytes_accessed=2 * nodes * images, transcendentals=0
        ),
        name="layer_more",
    )(place, rounded, own, diagonal, *[matrix] * count)


def read_back(place, ids, blocks, keys, parts, node_dev, before, weight=1):
    slots = ids.shape[0]
    height, images = blocks[0].shape

    def body(place_ref, ids_ref, *refs):
        out, both = refs[-2:]
        lane = lax.broadcasted_iota(jnp.int32, (slots, height), 1)
        picks = []
        for row, (key, part) in enumerate(keys):
            store_halves(refs[row][...], both, row * height)
            node = (place_ref[0] ^ key) * node_dev + part * height + lane
            picks.append(jnp.where(ids_ref[...] == node, 1.0, 0.0).astype(jnp.bfloat16))
        total = jnp.dot(jnp.concatenate(picks, axis=1), both[...], preferred_element_type=jnp.float32)
        total = (total[:, :images] + total[:, images:]) * (1.0 / RESULT_SCALE)
        if before is not None:
            total = total + refs[len(blocks)][...]
        out[...] = total

    more = [] if before is None else [before]
    vmem = pl.BlockSpec(memory_space=pltpu.VMEM)
    return pl.pallas_call(
        body,
        in_specs=[pl.BlockSpec(memory_space=pltpu.SMEM)] + [vmem] * (1 + len(blocks) + len(more)),
        out_shape=jax.ShapeDtypeStruct((slots, images), jnp.float32),
        scratch_shapes=[pltpu.VMEM((len(blocks) * height, 2 * images), jnp.bfloat16)],
        compiler_params=pltpu.CompilerParams(vmem_limit_bytes=(8 + 2 * len(blocks)) * MIB),
        cost_estimate=pl.CostEstimate(
            flops=weight * 4 * len(blocks) * height * slots * images,
            bytes_accessed=8 * slots * images,
            transcendentals=0,
        ),
        name="read_back",
    )(place, ids, *blocks, *more)


def on_device(trace_parts, node_slab, node_local, solid_fraction, influence):
    node_dev = solid_fraction.shape[1]
    slots, images = trace_parts.shape
    wide_count = lax.axis_size("wide")
    narrow_count = lax.axis_size("narrow")
    nodes = wide_count * node_dev
    place = jnp.stack([lax.axis_index("wide"), lax.axis_index("narrow")]).astype(jnp.int32)
    ids = (node_slab[:, 0] * node_dev + node_local).reshape(-1, 1)
    diagonal = (solid_fraction - 1.0).reshape(-1, 1)
    matrix = influence.reshape(narrow_count * node_dev, nodes)
    barrier = lax.optimization_barrier

    parts = id_parts(node_slab[:, 0], node_local, nodes, node_dev)
    sent = with_ids(trace_parts * TRACE_SCALE, parts)
    extra = sent.shape[0] - slots
    half = slots // 2
    held = gather_far((sent, (sent[: extra + half], sent[extra + half :])), True)

    held[3] = [exchange(held[2][0], "wide", 1)]

    def rows_of(key, part=None):
        if len(held[key]) == 1:
            data = held[key][0].astype(jnp.float32)
            return Rows(data, data, extra, (0, slots))
        tail = held[key][0].astype(jnp.float32)
        if part == 0:
            return Rows(tail, tail, extra, (0, half))
        return Rows(held[key][1].astype(jnp.float32), tail, 0, (half, slots))

    def add_up(rows, before):
        return scatter(rows, slots, before, nodes, node_dev)

    sums = add_up([rows_of(0), rows_of(1), rows_of(2)], None)
    held[4] = [after(held[4][0], sums)]
    held[5] = [exchange(held[4][0], "wide", 1)]
    held[7] = [exchange(held[6][0], "wide", 1)]
    sums = add_up([rows_of(3), rows_of(4), rows_of(6, 0)], sums)
    held[5], held[6][1], held[7][0], sums = barrier((held[5], held[6][1], held[7][0], sums))
    held[7].append(exchange(held[6][1], "wide", 1))
    sums = add_up([rows_of(5), rows_of(6, 1), rows_of(7, 0)], sums)
    held[7][1], sums = barrier((held[7][1], sums))
    step = 8
    while step < wide_count:
        for key in range(step):
            held[key ^ step] = [exchange(part, "wide", step) for part in held[key]]
        for key in range(step, 2 * step, 2):
            sums = add_up([rows_of(k, p) for k in (key, key + 1) for p in range(len(held[k]))], sums)
        step *= 2
    far = [k for k in range(narrow_count) if k >= 2]
    near = [k for k in range(narrow_count) if k < 2]
    jobs = [(k, 0) for k in far]
    rounded, own, *shares = scatter_and_layer(
        place, [rows_of(7, 1)], slots, sums, matrix, jobs, 2, nodes, node_dev
    )
    crossed = [exchange(share, "narrow", k) for share, (k, _) in zip(shares, jobs)]
    jobs = [(k, 0) for k in near] + [(k, 1) for k in far]
    shares = layer_more(place, rounded, own, matrix, diagonal, jobs, 2)
    *crossed, upper = barrier((*crossed, shares[0]))
    crossed += [exchange(share, "narrow", k) for share, (k, _) in zip(shares[1 : len(near)], jobs[1:])]
    crossed_more = [exchange(share, "narrow", k) for share, (k, _) in zip(shares[len(near) :], jobs[len(near) :])]
    shares = layer_more(place, rounded, own, matrix, diagonal, [(k, 1) for k in near], 2)
    *crossed, lower = barrier((*crossed, shares[0]))
    crossed_more += [exchange(share, "narrow", k) for share, k in zip(shares[1:], near[1:])]
    for part in crossed:
        upper = upper + part.astype(jnp.float32)
    sent = (upper * RESULT_SCALE).astype(jnp.float16)
    first = gather_far((sent, None), False)
    for part in crossed_more:
        lower = lower + part.astype(jnp.float32)
    sent = (lower * RESULT_SCALE).astype(jnp.float16)
    second = gather_far((sent, None), False)

    def look_up(keys, before, weight=1):
        blocks = [(first, second)[part][k][0].astype(jnp.float32) for k, part in keys]
        return read_back(place, ids, blocks, keys, 2, node_dev, before, weight)

    def both_parts(*keys):
        return [(k, part) for part in range(2) for k in keys]

    for held in (first, second):
        held[1], held[2] = [after(held[1][0], first[4][0])], [after(held[2][0], first[4][0])]
        held[3] = [exchange(held[2][0], "wide", 1)]
        held[5] = [exchange(held[4][0], "wide", 1)]
        held[7] = [exchange(held[6][0], "wide", 1)]
    found = look_up(both_parts(0, 1, 2), None, 1)
    found = look_up(both_parts(3, 4, 6), found)
    first[5], first[7], second[5], second[7], found = barrier((first[5], first[7], second[5], second[7], found))
    step = 8
    while step < wide_count:
        for held in (first, second):
            for key in range(step):
                held[key ^ step] = [exchange(held[key][0], "wide", step)]
        for key in range(step, 2 * step, 4):
            found = look_up(both_parts(*range(key, key + 4)), found)
        step *= 2
    dirichlet = look_up(both_parts(5, 7), found)
    potential = jnp.concatenate([upper, lower], axis=0)
    return (potential[None], dirichlet)


def solution(mesh):
    placed = (
        P(("wide", "narrow"), None),
        P(("wide", "narrow"), None),
        P(("wide", "narrow")),
        P("narrow", "wide"),
        P(None, "wide", "narrow", None),
    )
    return jax.shard_map(
        on_device,
        mesh=mesh,
        in_specs=placed,
        out_specs=(P("narrow", "wide", None), P(("wide", "narrow"), None)),
        check_vma=False,
    )
```

```python
import jax
import jax.numpy as jnp
from jax import lax
from jax.experimental import pallas as pl
from jax.experimental.pallas import tpu as pltpu
from jax.sharding import PartitionSpec as P

TRACE_SCALE = 2.0**13
RESULT_SCALE = 2.0
MIB = 2**20
ROWS = 8
EXACT = 2048


def exchange(block, axis, offset):
    count = lax.axis_size(axis)
    return lax.ppermute(block, axis, [(i, i ^ offset) for i in range(count)])


def after(value, *others):
    return lax.optimization_barrier((value, *others))[0]


def gather_far(parts, split):
    whole, pieces = parts
    held = {0: [whole]}
    held[4] = [exchange(whole, "wide", 4)]
    held[2] = [exchange(whole, "wide", 2)]
    held[1] = [exchange(whole, "wide", 1)]
    if split:
        held[6] = [exchange(pieces[0], "wide", 6), exchange(after(pieces[1], held[2][0]), "wide", 6)]
    else:
        held[6] = [exchange(whole, "wide", 6)]
    return held


def id_parts(slab, local, nodes, node_dev):
    return [slab * node_dev + local] if nodes <= EXACT else [slab, local]


def with_ids(values, parts):
    slots, images = values.shape
    per = -(-slots // images)
    extra = -(-len(parts) * per // ROWS) * ROWS
    total = jnp.pad(values, ((extra, 0), (0, 0)))
    for n, part in enumerate(parts):
        for r in range(per):
            piece = part.reshape(1, slots)[:, r * images : (r + 1) * images].astype(values.dtype)
            row = n * per + r
            total = total + jnp.pad(piece, ((row, extra + slots - row - 1), (0, images - piece.shape[1])))
    return total.astype(jnp.float16)


def ids_of(tail, slots, nodes, node_dev):
    images = tail.shape[1]
    per = -(-slots // images)

    def line(first):
        pieces = [tail[first + r : first + r + 1, : min(images, slots - r * images)] for r in range(per)]
        return pieces[0] if per == 1 else jnp.concatenate(pieces, axis=1)

    return (line(0) if nodes <= EXACT else line(0) * node_dev + line(per)).astype(jnp.int32)


def store_halves(values, out, first):
    rows, images = values.shape
    high = values.astype(jnp.bfloat16)
    out[first : first + rows, :images] = high
    out[first : first + rows, images:] = (values - high.astype(jnp.float32)).astype(jnp.bfloat16)


def cost(flops, moved, weight):
    return pl.CostEstimate(flops=int(flops * weight) + 1, bytes_accessed=int(moved * weight) + 1, transcendentals=0)


class Rows:
    def __init__(self, data, tail, first, span):
        self.data, self.tail, self.first, self.span = data, tail, first, span
        self.count = span[1] - span[0]


def row_specs(rows):
    return [pl.BlockSpec(memory_space=pltpu.VMEM)] * (2 * len(rows))


def row_args(rows):
    return [array for part in rows for array in (part.data, part.tail)]


def scatter_tile(rows, refs, both, first_node, tile, slots, nodes, node_dev):
    @pl.when(first_node == 0)
    def _():
        done = 0
        for part, data in zip(rows, refs[::2]):
            store_halves(data[part.first : part.first + part.count, :], both, done)
            done += part.count

    picks = []
    for part, tail in zip(rows, refs[1::2]):
        node = first_node + lax.broadcasted_iota(jnp.int32, (tile, part.count), 0)
        ids = ids_of(tail, slots, nodes, node_dev)[:, part.span[0] : part.span[1]]
        picks.append(jnp.where(ids == node, 1.0, 0.0).astype(jnp.bfloat16))
    total = jnp.dot(jnp.concatenate(picks, axis=1), both[...], preferred_element_type=jnp.float32)
    images = total.shape[1] // 2
    return total[:, :images] + total[:, images:]


def scatter(rows, slots, before, nodes, node_dev, weight):
    images = rows[0].data.shape[1]
    tile = 2 * node_dev
    depth = sum(part.count for part in rows)

    def body(*refs):
        out, both = refs[-2:]
        total = scatter_tile(rows, refs[: 2 * len(rows)], both, pl.program_id(0) * tile, tile, slots, nodes, node_dev)
        if before is not None:
            total = total + refs[2 * len(rows)][...]
        out[...] = total

    part = pl.BlockSpec((tile, images), lambda s: (s, 0))
    more = [] if before is None else [before]
    return pl.pallas_call(
        body,
        grid=(nodes // tile,),
        in_specs=row_specs(rows) + [part] * len(more),
        out_specs=part,
        out_shape=jax.ShapeDtypeStruct((nodes, images), jnp.float32),
        scratch_shapes=[pltpu.VMEM((depth, 2 * images), jnp.bfloat16)],
        compiler_params=pltpu.CompilerParams(vmem_limit_bytes=(8 + 2 * -(-depth // slots)) * MIB),
        cost_estimate=cost(4 * depth * nodes * images, 8 * nodes * images, weight),
        name="scatter_traces",
    )(*row_args(rows), *more)


def row_block(place_ref, job, parts):
    offset, part = job
    return (place_ref[1] ^ offset) * parts + part


def scatter_and_layer(place, rows, slots, before, matrix, jobs, parts, nodes, node_dev, weight):
    images = rows[0].data.shape[1]
    tile = 2 * node_dev
    steps = nodes // tile
    depth = sum(part.count for part in rows)
    count = len(jobs)
    height = node_dev // parts

    def body(place_ref, *refs):
        before_ref, matrix_ref = refs[2 * len(rows) : 2 * len(rows) + 2]
        rounded, own = refs[2 * len(rows) + 2 : 2 * len(rows) + 4]
        outs = refs[2 * len(rows) + 4 : -3]
        both, matrix_held, sems = refs[-3:]
        step = pl.program_id(0)
        fetches = []
        for n, job in enumerate(jobs):
            first = pl.multiple_of(row_block(place_ref, job, parts) * height, height)
            fetches.append(
                pltpu.make_async_copy(matrix_ref.at[pl.ds(first, height), :], matrix_held.at[n], sems.at[n])
            )

        @pl.when(step == 0)
        def _():
            for fetch in fetches:
                fetch.start()

        total = scatter_tile(rows, refs[: 2 * len(rows)], both, step * tile, tile, slots, nodes, node_dev)
        total = (total + before_ref[...]) * (1.0 / TRACE_SCALE)
        for half in range(2):
            @pl.when(2 * step + half == place_ref[0])
            def _():
                own[...] = total[half * node_dev : (half + 1) * node_dev, :]

        rounded[pl.ds(pl.multiple_of(step * tile, tile), tile), :] = total.astype(jnp.bfloat16)

        @pl.when(step == steps - 1)
        def _():
            for n, fetch in enumerate(fetches):
                fetch.wait()
                layer = jnp.dot(matrix_held[n], rounded[...], preferred_element_type=jnp.float32)
                outs[n][...] = layer.astype(outs[n].dtype)

    one = pl.BlockSpec((height, images), lambda s, p: (0, 0))
    limit = 10 + 2 * -(-depth // slots) + (2 * count * height * nodes + 4 * nodes * images) // MIB
    return pl.pallas_call(
        body,
        grid_spec=pltpu.PrefetchScalarGridSpec(
            num_scalar_prefetch=1,
            grid=(steps,),
            in_specs=row_specs(rows)
            + [pl.BlockSpec((tile, images), lambda s, p: (s, 0)), pl.BlockSpec(memory_space=pl.ANY)],
            out_specs=[
                pl.BlockSpec((nodes, images), lambda s, p: (0, 0)),
                pl.BlockSpec((node_dev, images), lambda s, p: (0, 0)),
            ]
            + [one] * count,
            scratch_shapes=[
                pltpu.VMEM((depth, 2 * images), jnp.bfloat16),
                pltpu.VMEM((count, height, nodes), matrix.dtype),
                pltpu.SemaphoreType.DMA((count,)),
            ],
        ),
        out_shape=[
            jax.ShapeDtypeStruct((nodes, images), jnp.bfloat16),
            jax.ShapeDtypeStruct((node_dev, images), jnp.float32),
        ]
        + [jax.ShapeDtypeStruct((height, images), jnp.bfloat16)] * count,
        compiler_params=pltpu.CompilerParams(vmem_limit_bytes=limit * MIB),
        cost_estimate=cost(
            (4 * depth + 2 * count * height) * nodes * images, 8 * nodes * images, weight
        ),
        name="scatter_and_layer",
    )(place, *row_args(rows), before, matrix)


def layer_more(place, rounded, own, matrix, diagonal, jobs, parts, weight):
    node_dev, images = own.shape
    nodes = rounded.shape[0]
    count = len(jobs)
    height = node_dev // parts

    def body(place_ref, rounded_ref, own_ref, diagonal_ref, *refs):
        for n, (offset, part) in enumerate(jobs):
            layer = jnp.dot(refs[n][...], rounded_ref[...], preferred_element_type=jnp.float32)
            if offset == 0:
                here = slice(part * height, (part + 1) * height)
                layer = layer + diagonal_ref[here, :] * own_ref[here, :]
            refs[count + n][...] = layer.astype(refs[count + n].dtype)

    def spec(array):
        return pl.BlockSpec(array.shape, lambda i, p: (0, 0))

    return pl.pallas_call(
        body,
        grid_spec=pltpu.PrefetchScalarGridSpec(
            num_scalar_prefetch=1,
            grid=(1,),
            in_specs=[spec(rounded), spec(own), spec(diagonal)]
            + [pl.BlockSpec((height, nodes), lambda i, p, job=job: (row_block(p, job, parts), 0)) for job in jobs],
            out_specs=[pl.BlockSpec((height, images), lambda i, p: (0, 0))] * count,
        ),
        out_shape=[
            jax.ShapeDtypeStruct((height, images), jnp.float32 if offset == 0 else jnp.bfloat16)
            for offset, _ in jobs
        ],
        compiler_params=pltpu.CompilerParams(
            vmem_limit_bytes=(8 + (4 * nodes * images + 4 * count * height * nodes) // MIB) * MIB
        ),
        cost_estimate=cost(2 * count * height * nodes * images, 2 * nodes * images, weight),
        name="layer_more",
    )(place, rounded, own, diagonal, *[matrix] * count)


def read_back(place, ids, blocks, keys, parts, node_dev, before, weight):
    slots = ids.shape[0]
    height, images = blocks[0].shape

    def body(place_ref, ids_ref, *refs):
        out, both = refs[-2:]
        lane = lax.broadcasted_iota(jnp.int32, (slots, height), 1)
        picks = []
        for row, (key, part) in enumerate(keys):
            store_halves(refs[row][...], both, row * height)
            node = (place_ref[0] ^ key) * node_dev + part * height + lane
            picks.append(jnp.where(ids_ref[...] == node, 1.0, 0.0).astype(jnp.bfloat16))
        total = jnp.dot(jnp.concatenate(picks, axis=1), both[...], preferred_element_type=jnp.float32)
        total = (total[:, :images] + total[:, images:]) * (1.0 / RESULT_SCALE)
        if before is not None:
            total = total + refs[len(blocks)][...]
        out[...] = total

    more = [] if before is None else [before]
    vmem = pl.BlockSpec(memory_space=pltpu.VMEM)
    return pl.pallas_call(
        body,
        in_specs=[pl.BlockSpec(memory_space=pltpu.SMEM)] + [vmem] * (1 + len(blocks) + len(more)),
        out_shape=jax.ShapeDtypeStruct((slots, images), jnp.float32),
        scratch_shapes=[pltpu.VMEM((len(blocks) * height, 2 * images), jnp.bfloat16)],
        compiler_params=pltpu.CompilerParams(vmem_limit_bytes=(8 + 2 * len(blocks)) * MIB),
        cost_estimate=cost(4 * len(blocks) * height * slots * images, 8 * slots * images, weight),
        name="read_back",
    )(place, ids, *blocks, *more)


def on_device(trace_parts, node_slab, node_local, solid_fraction, influence):
    node_dev = solid_fraction.shape[1]
    slots, images = trace_parts.shape
    wide_count = lax.axis_size("wide")
    narrow_count = lax.axis_size("narrow")
    nodes = wide_count * node_dev
    place = jnp.stack([lax.axis_index("wide"), lax.axis_index("narrow")]).astype(jnp.int32)
    diagonal = (solid_fraction - 1.0).reshape(-1, 1)
    matrix = influence.reshape(narrow_count * node_dev, nodes)
    barrier = lax.optimization_barrier

    slab = barrier(node_slab.reshape(slots))
    parts = id_parts(slab, node_local, nodes, node_dev)
    sent = with_ids(trace_parts * TRACE_SCALE, parts)
    extra = sent.shape[0] - slots
    half = slots // 2
    held = gather_far((sent, (sent[: extra + half], sent[extra + half :])), True)

    held[3] = [exchange(held[2][0], "wide", 1)]

    def rows_of(key, part=None):
        if len(held[key]) == 1:
            data = held[key][0].astype(jnp.float32)
            return Rows(data, data, extra, (0, slots))
        tail = held[key][0].astype(jnp.float32)
        if part == 0:
            return Rows(tail, tail, extra, (0, half))
        return Rows(held[key][1].astype(jnp.float32), tail, 0, (half, slots))

    def add_up(rows, before, weight=1):
        return scatter(rows, slots, before, nodes, node_dev, weight)

    sums = add_up([rows_of(0), rows_of(1), rows_of(2)], None, 1)
    held[4] = [after(held[4][0], sums)]
    held[5] = [exchange(held[4][0], "wide", 1)]
    held[7] = [exchange(held[6][0], "wide", 1)]
    sums = add_up([rows_of(3), rows_of(4), rows_of(6, 0)], sums, 1)
    held[5], held[6][1], held[7][0], sums = barrier((held[5], held[6][1], held[7][0], sums))
    held[7].append(exchange(held[6][1], "wide", 1))
    sums = add_up([rows_of(5), rows_of(6, 1), rows_of(7, 0)], sums, 1)
    held[7][1], sums = barrier((held[7][1], sums))
    step = 8
    while step < wide_count:
        for key in range(step):
            held[key ^ step] = [exchange(part, "wide", step) for part in held[key]]
        for key in range(step, 2 * step, 2):
            sums = add_up([rows_of(k, p) for k in (key, key + 1) for p in range(len(held[k]))], sums)
        step *= 2
    slab, local, sums = barrier((slab, node_local, sums))
    ids = (slab * node_dev + local).reshape(-1, 1)
    far = [k for k in range(narrow_count) if k >= 2]
    near = [k for k in range(narrow_count) if k < 2]
    jobs = [(k, 0) for k in far]
    rounded, own, *shares = scatter_and_layer(
        place, [rows_of(7, 1)], slots, sums, matrix, jobs, 2, nodes, node_dev, 1
    )
    crossed = [exchange(share, "narrow", k) for share, (k, _) in zip(shares, jobs)]
    jobs = [(k, 0) for k in near] + [(k, 1) for k in far]
    shares = layer_more(place, rounded, own, matrix, diagonal, jobs, 2, 1)
    *crossed, upper = barrier((*crossed, shares[0]))
    crossed += [exchange(share, "narrow", k) for share, (k, _) in zip(shares[1 : len(near)], jobs[1:])]
    crossed_more = [exchange(share, "narrow", k) for share, (k, _) in zip(shares[len(near) :], jobs[len(near) :])]
    shares = layer_more(place, rounded, own, matrix, diagonal, [(k, 1) for k in near], 2, 1)
    *crossed, lower = barrier((*crossed, shares[0]))
    crossed_more += [exchange(share, "narrow", k) for share, k in zip(shares[1:], near[1:])]
    for part in crossed:
        upper = upper + part.astype(jnp.float32)
    sent = (upper * RESULT_SCALE).astype(jnp.float16)
    first = gather_far((sent, None), False)
    for part in crossed_more:
        lower = lower + part.astype(jnp.float32)
    sent = (lower * RESULT_SCALE).astype(jnp.float16)
    second = gather_far((sent, None), False)

    def look_up(keys, before, weight=1):
        blocks = [(first, second)[part][k][0].astype(jnp.float32) for k, part in keys]
        return read_back(place, ids, blocks, keys, 2, node_dev, before, weight)

    def both_parts(*keys):
        return [(k, part) for part in range(2) for k in keys]

    far4, far6 = first[4][0], first[6][0]
    first[4] = [after(far4, first[1][0], second[1][0])]
    first[2], second[2] = [after(first[2][0], far4, far6)], [after(second[2][0], far4, far6)]
    for held in (first, second):
        held[3] = [exchange(held[2][0], "wide", 1)]
        held[5] = [exchange(held[4][0], "wide", 1)]
        held[7] = [exchange(held[6][0], "wide", 1)]
    found = look_up(both_parts(0, 1, 2), None, 0)
    found = look_up(both_parts(3, 4, 6) + [(5, 0), (7, 0)], found, 0)
    second[5], second[7], found = barrier((second[5], second[7], found))
    step = 8
    while step < wide_count:
        for held in (first, second):
            for key in range(step):
                held[key ^ step] = [exchange(held[key][0], "wide", step)]
        for key in range(step, 2 * step, 4):
            found = look_up(both_parts(*range(key, key + 4)), found)
        step *= 2
    dirichlet = look_up([(5, 1), (7, 1)], found)
    potential = jnp.concatenate([upper, lower], axis=0)
    return (potential[None], dirichlet)


def solution(mesh):
    placed = (
        P(("wide", "narrow"), None),
        P(("wide", "narrow"), None),
        P(("wide", "narrow")),
        P("narrow", "wide"),
        P(None, "wide", "narrow", None),
    )
    return jax.shard_map(
        on_device,
        mesh=mesh,
        in_specs=placed,
        out_specs=(P("narrow", "wide", None), P(("wide", "narrow"), None)),
        check_vma=False,
    )
```

```python
import jax
import jax.numpy as jnp
from jax import lax
from jax.experimental import pallas as pl
from jax.experimental.pallas import tpu as pltpu
from jax.sharding import PartitionSpec as P

TRACE_SCALE = 2.0**13
RESULT_SCALE = 2.0
MIB = 2**20
ROWS = 8
EXACT = 2048


def exchange(block, axis, offset):
    count = lax.axis_size(axis)
    return lax.ppermute(block, axis, [(i, i ^ offset) for i in range(count)])


def after(value, *others):
    return lax.optimization_barrier((value, *others))[0]


def gather_far(parts, split):
    whole, pieces = parts
    held = {0: [whole]}
    held[4] = [exchange(whole, "wide", 4)]
    held[2] = [exchange(whole, "wide", 2)]
    held[1] = [exchange(whole, "wide", 1)]
    if split:
        held[6] = [exchange(pieces[0], "wide", 6), exchange(after(pieces[1], held[2][0]), "wide", 6)]
    else:
        held[6] = [exchange(whole, "wide", 6)]
    return held


def id_parts(slab, local, nodes, node_dev):
    return [slab * node_dev + local] if nodes <= EXACT else [slab, local]


def with_ids(values, parts):
    slots, images = values.shape
    per = -(-slots // images)
    extra = -(-len(parts) * per // ROWS) * ROWS
    total = jnp.pad(values, ((extra, 0), (0, 0)))
    for n, part in enumerate(parts):
        for r in range(per):
            piece = part.reshape(1, slots)[:, r * images : (r + 1) * images].astype(values.dtype)
            row = n * per + r
            total = total + jnp.pad(piece, ((row, extra + slots - row - 1), (0, images - piece.shape[1])))
    return total.astype(jnp.float16)


def ids_of(tail, slots, nodes, node_dev):
    images = tail.shape[1]
    per = -(-slots // images)

    def line(first):
        pieces = [tail[first + r : first + r + 1, : min(images, slots - r * images)] for r in range(per)]
        return pieces[0] if per == 1 else jnp.concatenate(pieces, axis=1)

    return (line(0) if nodes <= EXACT else line(0) * node_dev + line(per)).astype(jnp.int32)


def store_halves(values, out, first):
    rows, images = values.shape
    high = values.astype(jnp.bfloat16)
    out[first : first + rows, :images] = high
    out[first : first + rows, images:] = (values - high.astype(jnp.float32)).astype(jnp.bfloat16)


def cost(flops, moved, weight):
    return pl.CostEstimate(flops=int(flops * weight) + 1, bytes_accessed=int(moved * weight) + 1, transcendentals=0)


class Rows:
    def __init__(self, data, tail, first, span):
        self.data, self.tail, self.first, self.span = data, tail, first, span
        self.count = span[1] - span[0]


def row_specs(rows):
    return [pl.BlockSpec(memory_space=pltpu.VMEM)] * (2 * len(rows))


def row_args(rows):
    return [array for part in rows for array in (part.data, part.tail)]


def scatter_tile(rows, refs, both, first_node, tile, slots, nodes, node_dev):
    @pl.when(first_node == 0)
    def _():
        done = 0
        for part, data in zip(rows, refs[::2]):
            store_halves(data[part.first : part.first + part.count, :], both, done)
            done += part.count

    picks = []
    for part, tail in zip(rows, refs[1::2]):
        node = first_node + lax.broadcasted_iota(jnp.int32, (tile, part.count), 0)
        ids = ids_of(tail, slots, nodes, node_dev)[:, part.span[0] : part.span[1]]
        picks.append(jnp.where(ids == node, 1.0, 0.0).astype(jnp.bfloat16))
    total = jnp.dot(jnp.concatenate(picks, axis=1), both[...], preferred_element_type=jnp.float32)
    images = total.shape[1] // 2
    return total[:, :images] + total[:, images:]


def scatter(rows, slots, before, nodes, node_dev, weight):
    images = rows[0].data.shape[1]
    tile = 4 * node_dev
    depth = sum(part.count for part in rows)

    def body(*refs):
        out, both = refs[-2:]
        total = scatter_tile(rows, refs[: 2 * len(rows)], both, pl.program_id(0) * tile, tile, slots, nodes, node_dev)
        if before is not None:
            total = total + refs[2 * len(rows)][...]
        out[...] = total

    part = pl.BlockSpec((tile, images), lambda s: (s, 0))
    more = [] if before is None else [before]
    return pl.pallas_call(
        body,
        grid=(nodes // tile,),
        in_specs=row_specs(rows) + [part] * len(more),
        out_specs=part,
        out_shape=jax.ShapeDtypeStruct((nodes, images), jnp.float32),
        scratch_shapes=[pltpu.VMEM((depth, 2 * images), jnp.bfloat16)],
        compiler_params=pltpu.CompilerParams(vmem_limit_bytes=(14 + 2 * -(-depth // slots)) * MIB),
        cost_estimate=cost(4 * depth * nodes * images, 8 * nodes * images, weight),
        name="scatter_traces",
    )(*row_args(rows), *more)


def row_block(place_ref, job, parts):
    offset, part = job
    return (place_ref[1] ^ offset) * parts + part


def scatter_and_layer(place, rows, slots, before, matrix, jobs, parts, nodes, node_dev, weight):
    images = rows[0].data.shape[1]
    tile = 4 * node_dev
    steps = nodes // tile
    depth = sum(part.count for part in rows)
    count = len(jobs)
    height = node_dev // parts

    def body(place_ref, *refs):
        before_ref, matrix_ref = refs[2 * len(rows) : 2 * len(rows) + 2]
        rounded, own = refs[2 * len(rows) + 2 : 2 * len(rows) + 4]
        outs = refs[2 * len(rows) + 4 : -3]
        both, matrix_held, sems = refs[-3:]
        step = pl.program_id(0)
        fetches = []
        for n, job in enumerate(jobs):
            first = pl.multiple_of(row_block(place_ref, job, parts) * height, height)
            fetches.append(
                pltpu.make_async_copy(matrix_ref.at[pl.ds(first, height), :], matrix_held.at[n], sems.at[n])
            )

        @pl.when(step == 0)
        def _():
            for fetch in fetches:
                fetch.start()

        total = scatter_tile(rows, refs[: 2 * len(rows)], both, step * tile, tile, slots, nodes, node_dev)
        total = (total + before_ref[...]) * (1.0 / TRACE_SCALE)
        for slab in range(tile // node_dev):
            @pl.when(tile // node_dev * step + slab == place_ref[0])
            def _():
                own[...] = total[slab * node_dev : (slab + 1) * node_dev, :]

        rounded[pl.ds(pl.multiple_of(step * tile, tile), tile), :] = total.astype(jnp.bfloat16)

        @pl.when(step == steps - 1)
        def _():
            for n, fetch in enumerate(fetches):
                fetch.wait()
                layer = jnp.dot(matrix_held[n], rounded[...], preferred_element_type=jnp.float32)
                outs[n][...] = layer.astype(outs[n].dtype)

    one = pl.BlockSpec((height, images), lambda s, p: (0, 0))
    limit = 16 + 2 * -(-depth // slots) + (2 * count * height * nodes + 4 * nodes * images) // MIB
    return pl.pallas_call(
        body,
        grid_spec=pltpu.PrefetchScalarGridSpec(
            num_scalar_prefetch=1,
            grid=(steps,),
            in_specs=row_specs(rows)
            + [pl.BlockSpec((tile, images), lambda s, p: (s, 0)), pl.BlockSpec(memory_space=pl.ANY)],
            out_specs=[
                pl.BlockSpec((nodes, images), lambda s, p: (0, 0)),
                pl.BlockSpec((node_dev, images), lambda s, p: (0, 0)),
            ]
            + [one] * count,
            scratch_shapes=[
                pltpu.VMEM((depth, 2 * images), jnp.bfloat16),
                pltpu.VMEM((count, height, nodes), matrix.dtype),
                pltpu.SemaphoreType.DMA((count,)),
            ],
        ),
        out_shape=[
            jax.ShapeDtypeStruct((nodes, images), jnp.bfloat16),
            jax.ShapeDtypeStruct((node_dev, images), jnp.float32),
        ]
        + [jax.ShapeDtypeStruct((height, images), jnp.bfloat16)] * count,
        compiler_params=pltpu.CompilerParams(vmem_limit_bytes=limit * MIB),
        cost_estimate=cost(
            (4 * depth + 2 * count * height) * nodes * images, 8 * nodes * images, weight
        ),
        name="scatter_and_layer",
    )(place, *row_args(rows), before, matrix)


def layer_more(place, rounded, own, matrix, diagonal, jobs, parts, weight):
    node_dev, images = own.shape
    nodes = rounded.shape[0]
    count = len(jobs)
    height = node_dev // parts

    def body(place_ref, rounded_ref, own_ref, diagonal_ref, *refs):
        for n, (offset, part) in enumerate(jobs):
            layer = jnp.dot(refs[n][...], rounded_ref[...], preferred_element_type=jnp.float32)
            if offset == 0:
                here = slice(part * height, (part + 1) * height)
                layer = layer + diagonal_ref[here, :] * own_ref[here, :]
            refs[count + n][...] = layer.astype(refs[count + n].dtype)

    def spec(array):
        return pl.BlockSpec(array.shape, lambda i, p: (0, 0))

    return pl.pallas_call(
        body,
        grid_spec=pltpu.PrefetchScalarGridSpec(
            num_scalar_prefetch=1,
            grid=(1,),
            in_specs=[spec(rounded), spec(own), spec(diagonal)]
            + [pl.BlockSpec((height, nodes), lambda i, p, job=job: (row_block(p, job, parts), 0)) for job in jobs],
            out_specs=[pl.BlockSpec((height, images), lambda i, p: (0, 0))] * count,
        ),
        out_shape=[
            jax.ShapeDtypeStruct((height, images), jnp.float32 if offset == 0 else jnp.bfloat16)
            for offset, _ in jobs
        ],
        compiler_params=pltpu.CompilerParams(
            vmem_limit_bytes=(8 + (4 * nodes * images + 4 * count * height * nodes) // MIB) * MIB
        ),
        cost_estimate=cost(2 * count * height * nodes * images, 2 * nodes * images, weight),
        name="layer_more",
    )(place, rounded, own, diagonal, *[matrix] * count)


def read_back(place, ids, blocks, keys, parts, node_dev, before, weight):
    slots = ids.shape[0]
    height, images = blocks[0].shape

    def body(place_ref, ids_ref, *refs):
        out, both = refs[-2:]
        lane = lax.broadcasted_iota(jnp.int32, (slots, height), 1)
        picks = []
        for row, (key, part) in enumerate(keys):
            store_halves(refs[row][...], both, row * height)
            node = (place_ref[0] ^ key) * node_dev + part * height + lane
            picks.append(jnp.where(ids_ref[...] == node, 1.0, 0.0).astype(jnp.bfloat16))
        total = jnp.dot(jnp.concatenate(picks, axis=1), both[...], preferred_element_type=jnp.float32)
        total = (total[:, :images] + total[:, images:]) * (1.0 / RESULT_SCALE)
        if before is not None:
            total = total + refs[len(blocks)][...]
        out[...] = total

    more = [] if before is None else [before]
    vmem = pl.BlockSpec(memory_space=pltpu.VMEM)
    return pl.pallas_call(
        body,
        in_specs=[pl.BlockSpec(memory_space=pltpu.SMEM)] + [vmem] * (1 + len(blocks) + len(more)),
        out_shape=jax.ShapeDtypeStruct((slots, images), jnp.float32),
        scratch_shapes=[pltpu.VMEM((len(blocks) * height, 2 * images), jnp.bfloat16)],
        compiler_params=pltpu.CompilerParams(vmem_limit_bytes=(8 + 2 * len(blocks)) * MIB),
        cost_estimate=cost(4 * len(blocks) * height * slots * images, 8 * slots * images, weight),
        name="read_back",
    )(place, ids, *blocks, *more)


def on_device(trace_parts, node_slab, node_local, solid_fraction, influence):
    node_dev = solid_fraction.shape[1]
    slots, images = trace_parts.shape
    wide_count = lax.axis_size("wide")
    narrow_count = lax.axis_size("narrow")
    nodes = wide_count * node_dev
    place = jnp.stack([lax.axis_index("wide"), lax.axis_index("narrow")]).astype(jnp.int32)
    diagonal = (solid_fraction - 1.0).reshape(-1, 1)
    matrix = influence.reshape(narrow_count * node_dev, nodes)
    barrier = lax.optimization_barrier

    slab = barrier(node_slab.reshape(slots))
    parts = id_parts(slab, node_local, nodes, node_dev)
    sent = with_ids(trace_parts * TRACE_SCALE, parts)
    extra = sent.shape[0] - slots
    half = slots // 2
    held = gather_far((sent, (sent[: extra + half], sent[extra + half :])), True)

    held[3] = [exchange(held[2][0], "wide", 1)]

    def rows_of(key, part=None):
        if len(held[key]) == 1:
            data = held[key][0].astype(jnp.float32)
            return Rows(data, data, extra, (0, slots))
        tail = held[key][0].astype(jnp.float32)
        if part == 0:
            return Rows(tail, tail, extra, (0, half))
        return Rows(held[key][1].astype(jnp.float32), tail, 0, (half, slots))

    def add_up(rows, before, weight=1):
        return scatter(rows, slots, before, nodes, node_dev, weight)

    sums = add_up([rows_of(0), rows_of(1), rows_of(2)], None, 1)
    held[4] = [after(held[4][0], sums)]
    held[5] = [exchange(held[4][0], "wide", 1)]
    held[7] = [exchange(held[6][0], "wide", 1)]
    sums = add_up([rows_of(3), rows_of(4), rows_of(6, 0)], sums, 1)
    held[5], held[6][1], held[7][0], sums = barrier((held[5], held[6][1], held[7][0], sums))
    held[7].append(exchange(held[6][1], "wide", 1))
    sums = add_up([rows_of(5), rows_of(6, 1), rows_of(7, 0)], sums, 1)
    held[7][1], sums = barrier((held[7][1], sums))
    step = 8
    while step < wide_count:
        for key in range(step):
            held[key ^ step] = [exchange(part, "wide", step) for part in held[key]]
        for key in range(step, 2 * step, 2):
            sums = add_up([rows_of(k, p) for k in (key, key + 1) for p in range(len(held[k]))], sums)
        step *= 2
    slab, local, sums = barrier((slab, node_local, sums))
    ids = (slab * node_dev + local).reshape(-1, 1)
    far = [k for k in range(narrow_count) if k >= 2]
    near = [k for k in range(narrow_count) if k < 2]
    jobs = [(k, 0) for k in far]
    rounded, own, *shares = scatter_and_layer(
        place, [rows_of(7, 1)], slots, sums, matrix, jobs, 2, nodes, node_dev, 1
    )
    crossed = [exchange(share, "narrow", k) for share, (k, _) in zip(shares, jobs)]
    jobs = [(k, 0) for k in near] + [(k, 1) for k in far]
    shares = layer_more(place, rounded, own, matrix, diagonal, jobs, 2, 1)
    *crossed, upper = barrier((*crossed, shares[0]))
    crossed += [exchange(share, "narrow", k) for share, (k, _) in zip(shares[1 : len(near)], jobs[1:])]
    crossed_more = [exchange(share, "narrow", k) for share, (k, _) in zip(shares[len(near) :], jobs[len(near) :])]
    shares = layer_more(place, rounded, own, matrix, diagonal, [(k, 1) for k in near], 2, 1)
    *crossed, lower = barrier((*crossed, shares[0]))
    crossed_more += [exchange(share, "narrow", k) for share, k in zip(shares[1:], near[1:])]
    for part in crossed:
        upper = upper + part.astype(jnp.float32)
    sent = (upper * RESULT_SCALE).astype(jnp.float16)
    first = gather_far((sent, None), False)
    for part in crossed_more:
        lower = lower + part.astype(jnp.float32)
    sent = (lower * RESULT_SCALE).astype(jnp.float16)
    second = gather_far((sent, None), False)

    def look_up(keys, before, weight=1):
        blocks = [(first, second)[part][k][0].astype(jnp.float32) for k, part in keys]
        return read_back(place, ids, blocks, keys, 2, node_dev, before, weight)

    def both_parts(*keys):
        return [(k, part) for part in range(2) for k in keys]

    far4, far6 = first[4][0], first[6][0]
    first[4] = [after(far4, first[1][0], second[1][0])]
    first[2], second[2] = [after(first[2][0], far4, far6)], [after(second[2][0], far4, far6)]
    for held in (first, second):
        held[3] = [exchange(held[2][0], "wide", 1)]
        held[5] = [exchange(held[4][0], "wide", 1)]
        held[7] = [exchange(held[6][0], "wide", 1)]
    found = look_up(both_parts(0, 1, 2), None, 0)
    found = look_up(both_parts(3, 4, 6) + [(5, 0), (7, 0)], found, 0)
    second[5], second[7], found = barrier((second[5], second[7], found))
    step = 8
    while step < wide_count:
        for held in (first, second):
            for key in range(step):
                held[key ^ step] = [exchange(held[key][0], "wide", step)]
        for key in range(step, 2 * step, 4):
            found = look_up(both_parts(*range(key, key + 4)), found)
        step *= 2
    dirichlet = look_up([(5, 1), (7, 1)], found)
    potential = jnp.concatenate([upper, lower], axis=0)
    return (potential[None], dirichlet)


def solution(mesh):
    placed = (
        P(("wide", "narrow"), None),
        P(("wide", "narrow"), None),
        P(("wide", "narrow")),
        P("narrow", "wide"),
        P(None, "wide", "narrow", None),
    )
    return jax.shard_map(
        on_device,
        mesh=mesh,
        in_specs=placed,
        out_specs=(P("narrow", "wide", None), P(("wide", "narrow"), None)),
        check_vma=False,
    )
```

```python
import jax
import jax.numpy as jnp
from jax import lax
from jax.experimental import pallas as pl
from jax.experimental.pallas import tpu as pltpu
from jax.sharding import PartitionSpec as P

TRACE_SCALE = 2.0**13
RESULT_SCALE = 2.0
MIB = 2**20
ROWS = 8
EXACT = 2048


def exchange(block, axis, offset):
    count = lax.axis_size(axis)
    return lax.ppermute(block, axis, [(i, i ^ offset) for i in range(count)])


def after(value, *others):
    return lax.optimization_barrier((value, *others))[0]


def gather_far(parts, split):
    whole, pieces = parts
    held = {0: [whole]}
    held[4] = [exchange(whole, "wide", 4)]
    held[2] = [exchange(whole, "wide", 2)]
    held[1] = [exchange(whole, "wide", 1)]
    if split:
        held[6] = [exchange(pieces[0], "wide", 6), exchange(after(pieces[1], held[2][0]), "wide", 6)]
    else:
        held[6] = [exchange(whole, "wide", 6)]
    return held


def id_parts(slab, local, nodes, node_dev):
    return [slab * node_dev + local] if nodes <= EXACT else [slab, local]


def with_ids(values, parts):
    slots, images = values.shape
    per = -(-slots // images)
    extra = -(-len(parts) * per // ROWS) * ROWS
    total = jnp.pad(values, ((extra, 0), (0, 0)))
    for n, part in enumerate(parts):
        for r in range(per):
            piece = part.reshape(1, slots)[:, r * images : (r + 1) * images].astype(values.dtype)
            row = n * per + r
            total = total + jnp.pad(piece, ((row, extra + slots - row - 1), (0, images - piece.shape[1])))
    return total.astype(jnp.float16)


def ids_of(tail, slots, nodes, node_dev):
    images = tail.shape[1]
    per = -(-slots // images)

    def line(first):
        pieces = [tail[first + r : first + r + 1, : min(images, slots - r * images)] for r in range(per)]
        return pieces[0] if per == 1 else jnp.concatenate(pieces, axis=1)

    return (line(0) if nodes <= EXACT else line(0) * node_dev + line(per)).astype(jnp.int32)


def store_halves(values, out, first):
    rows, images = values.shape
    high = values.astype(jnp.bfloat16)
    out[first : first + rows, :images] = high
    out[first : first + rows, images:] = (values - high.astype(jnp.float32)).astype(jnp.bfloat16)


def cost(flops, moved, weight):
    return pl.CostEstimate(flops=int(flops * weight) + 1, bytes_accessed=int(moved * weight) + 1, transcendentals=0)


class Rows:
    def __init__(self, data, tail, first, span):
        self.data, self.tail, self.first, self.span = data, tail, first, span
        self.count = span[1] - span[0]


def row_specs(rows):
    return [pl.BlockSpec(memory_space=pltpu.VMEM)] * (2 * len(rows))


def row_args(rows):
    return [array for part in rows for array in (part.data, part.tail)]


def scatter_tile(rows, refs, both, first_node, tile, slots, nodes, node_dev):
    @pl.when(first_node == 0)
    def _():
        done = 0
        for part, data in zip(rows, refs[::2]):
            store_halves(data[part.first : part.first + part.count, :], both, done)
            done += part.count

    picks = []
    for part, tail in zip(rows, refs[1::2]):
        node = first_node + lax.broadcasted_iota(jnp.int32, (tile, part.count), 0)
        ids = ids_of(tail, slots, nodes, node_dev)[:, part.span[0] : part.span[1]]
        picks.append(jnp.where(ids == node, 1.0, 0.0).astype(jnp.bfloat16))
    total = jnp.dot(jnp.concatenate(picks, axis=1), both[...], preferred_element_type=jnp.float32)
    images = total.shape[1] // 2
    return total[:, :images] + total[:, images:]


def scatter(rows, slots, before, nodes, node_dev, weight):
    images = rows[0].data.shape[1]
    tile = 4 * node_dev
    depth = sum(part.count for part in rows)

    def body(*refs):
        out, both = refs[-2:]
        total = scatter_tile(rows, refs[: 2 * len(rows)], both, pl.program_id(0) * tile, tile, slots, nodes, node_dev)
        if before is not None:
            total = total + refs[2 * len(rows)][...]
        out[...] = total

    part = pl.BlockSpec((tile, images), lambda s: (s, 0))
    more = [] if before is None else [before]
    return pl.pallas_call(
        body,
        grid=(nodes // tile,),
        in_specs=row_specs(rows) + [part] * len(more),
        out_specs=part,
        out_shape=jax.ShapeDtypeStruct((nodes, images), jnp.float32),
        scratch_shapes=[pltpu.VMEM((depth, 2 * images), jnp.bfloat16)],
        compiler_params=pltpu.CompilerParams(vmem_limit_bytes=(14 + 2 * -(-depth // slots)) * MIB),
        cost_estimate=cost(4 * depth * nodes * images, 8 * nodes * images, weight),
        name="scatter_traces",
    )(*row_args(rows), *more)


def row_block(place_ref, job, parts):
    offset, part = job
    return (place_ref[1] ^ offset) * parts + part


def scatter_and_layer(place, rows, slots, before, matrix, jobs, parts, nodes, node_dev, weight):
    images = rows[0].data.shape[1]
    tile = 4 * node_dev
    steps = nodes // tile
    depth = sum(part.count for part in rows)
    count = len(jobs)
    height = node_dev // parts

    def body(place_ref, *refs):
        before_ref, matrix_ref = refs[2 * len(rows) : 2 * len(rows) + 2]
        rounded, own = refs[2 * len(rows) + 2 : 2 * len(rows) + 4]
        outs = refs[2 * len(rows) + 4 : -3]
        both, matrix_held, sems = refs[-3:]
        step = pl.program_id(0)
        fetches = []
        for n, job in enumerate(jobs):
            first = pl.multiple_of(row_block(place_ref, job, parts) * height, height)
            fetches.append(
                pltpu.make_async_copy(matrix_ref.at[pl.ds(first, height), :], matrix_held.at[n], sems.at[n])
            )

        @pl.when(step == 0)
        def _():
            for fetch in fetches:
                fetch.start()

        total = scatter_tile(rows, refs[: 2 * len(rows)], both, step * tile, tile, slots, nodes, node_dev)
        total = (total + before_ref[...]) * (1.0 / TRACE_SCALE)
        for slab in range(tile // node_dev):
            @pl.when(tile // node_dev * step + slab == place_ref[0])
            def _():
                own[...] = total[slab * node_dev : (slab + 1) * node_dev, :]

        rounded[pl.ds(pl.multiple_of(step * tile, tile), tile), :] = total.astype(jnp.bfloat16)

        @pl.when(step == steps - 1)
        def _():
            for n, fetch in enumerate(fetches):
                fetch.wait()
                layer = jnp.dot(matrix_held[n], rounded[...], preferred_element_type=jnp.float32)
                outs[n][...] = layer.astype(outs[n].dtype)

    one = pl.BlockSpec((height, images), lambda s, p: (0, 0))
    limit = 16 + 2 * -(-depth // slots) + (2 * count * height * nodes + 4 * nodes * images) // MIB
    return pl.pallas_call(
        body,
        grid_spec=pltpu.PrefetchScalarGridSpec(
            num_scalar_prefetch=1,
            grid=(steps,),
            in_specs=row_specs(rows)
            + [pl.BlockSpec((tile, images), lambda s, p: (s, 0)), pl.BlockSpec(memory_space=pl.ANY)],
            out_specs=[
                pl.BlockSpec((nodes, images), lambda s, p: (0, 0)),
                pl.BlockSpec((node_dev, images), lambda s, p: (0, 0)),
            ]
            + [one] * count,
            scratch_shapes=[
                pltpu.VMEM((depth, 2 * images), jnp.bfloat16),
                pltpu.VMEM((count, height, nodes), matrix.dtype),
                pltpu.SemaphoreType.DMA((count,)),
            ],
        ),
        out_shape=[
            jax.ShapeDtypeStruct((nodes, images), jnp.bfloat16),
            jax.ShapeDtypeStruct((node_dev, images), jnp.float32),
        ]
        + [jax.ShapeDtypeStruct((height, images), jnp.bfloat16)] * count,
        compiler_params=pltpu.CompilerParams(vmem_limit_bytes=limit * MIB),
        cost_estimate=cost(
            (4 * depth + 2 * count * height) * nodes * images, 8 * nodes * images, weight
        ),
        name="scatter_and_layer",
    )(place, *row_args(rows), before, matrix)


def layer_more(place, rounded, own, matrix, diagonal, jobs, parts, weight):
    node_dev, images = own.shape
    nodes = rounded.shape[0]
    count = len(jobs)
    height = node_dev // parts

    def body(place_ref, rounded_ref, own_ref, diagonal_ref, *refs):
        for n, (offset, part) in enumerate(jobs):
            layer = jnp.dot(refs[n][...], rounded_ref[...], preferred_element_type=jnp.float32)
            if offset == 0:
                here = slice(part * height, (part + 1) * height)
                layer = layer + diagonal_ref[here, :] * own_ref[here, :]
            refs[count + n][...] = layer.astype(refs[count + n].dtype)

    def spec(array):
        return pl.BlockSpec(array.shape, lambda i, p: (0, 0))

    return pl.pallas_call(
        body,
        grid_spec=pltpu.PrefetchScalarGridSpec(
            num_scalar_prefetch=1,
            grid=(1,),
            in_specs=[spec(rounded), spec(own), spec(diagonal)]
            + [pl.BlockSpec((height, nodes), lambda i, p, job=job: (row_block(p, job, parts), 0)) for job in jobs],
            out_specs=[pl.BlockSpec((height, images), lambda i, p: (0, 0))] * count,
        ),
        out_shape=[
            jax.ShapeDtypeStruct((height, images), jnp.float32 if offset == 0 else jnp.bfloat16)
            for offset, _ in jobs
        ],
        compiler_params=pltpu.CompilerParams(
            vmem_limit_bytes=(8 + (4 * nodes * images + 4 * count * height * nodes) // MIB) * MIB
        ),
        cost_estimate=cost(2 * count * height * nodes * images, 2 * nodes * images, weight),
        name="layer_more",
    )(place, rounded, own, diagonal, *[matrix] * count)


def read_back(place, ids, blocks, keys, parts, node_dev, before, weight):
    slots = ids.shape[0]
    height, images = blocks[0].shape

    def body(place_ref, ids_ref, *refs):
        out, both = refs[-2:]
        place_in = ids_ref[...] - lax.broadcasted_iota(jnp.int32, (slots, height), 1)
        picks = []
        for row, (key, part) in enumerate(keys):
            store_halves(refs[row][...], both, row * height)
            first = (place_ref[0] ^ key) * node_dev + part * height
            picks.append(jnp.where(place_in == first, 1.0, 0.0).astype(jnp.bfloat16))
        total = jnp.dot(jnp.concatenate(picks, axis=1), both[...], preferred_element_type=jnp.float32)
        total = (total[:, :images] + total[:, images:]) * (1.0 / RESULT_SCALE)
        if before is not None:
            total = total + refs[len(blocks)][...]
        out[...] = total

    more = [] if before is None else [before]
    vmem = pl.BlockSpec(memory_space=pltpu.VMEM)
    return pl.pallas_call(
        body,
        in_specs=[pl.BlockSpec(memory_space=pltpu.SMEM)] + [vmem] * (1 + len(blocks) + len(more)),
        out_shape=jax.ShapeDtypeStruct((slots, images), jnp.float32),
        scratch_shapes=[pltpu.VMEM((len(blocks) * height, 2 * images), jnp.bfloat16)],
        compiler_params=pltpu.CompilerParams(vmem_limit_bytes=(8 + 2 * len(blocks)) * MIB),
        cost_estimate=cost(4 * len(blocks) * height * slots * images, 8 * slots * images, weight),
        name="read_back",
    )(place, ids, *blocks, *more)


def on_device(trace_parts, node_slab, node_local, solid_fraction, influence):
    node_dev = solid_fraction.shape[1]
    slots, images = trace_parts.shape
    wide_count = lax.axis_size("wide")
    narrow_count = lax.axis_size("narrow")
    nodes = wide_count * node_dev
    place = jnp.stack([lax.axis_index("wide"), lax.axis_index("narrow")]).astype(jnp.int32)
    diagonal = (solid_fraction - 1.0).reshape(-1, 1)
    matrix = influence.reshape(narrow_count * node_dev, nodes)
    barrier = lax.optimization_barrier

    slab = barrier(node_slab.reshape(slots))
    parts = id_parts(slab, node_local, nodes, node_dev)
    sent = with_ids(trace_parts * TRACE_SCALE, parts)
    extra = sent.shape[0] - slots
    half = slots // 2
    held = gather_far((sent, (sent[: extra + half], sent[extra + half :])), True)

    held[3] = [exchange(held[2][0], "wide", 1)]

    def rows_of(key, part=None):
        if len(held[key]) == 1:
            data = held[key][0].astype(jnp.float32)
            return Rows(data, data, extra, (0, slots))
        tail = held[key][0].astype(jnp.float32)
        if part == 0:
            return Rows(tail, tail, extra, (0, half))
        return Rows(held[key][1].astype(jnp.float32), tail, 0, (half, slots))

    def add_up(rows, before, weight=1):
        return scatter(rows, slots, before, nodes, node_dev, weight)

    sums = add_up([rows_of(0), rows_of(1), rows_of(2)], None, 1)
    held[4] = [after(held[4][0], sums)]
    held[5] = [exchange(held[4][0], "wide", 1)]
    held[7] = [exchange(held[6][0], "wide", 1)]
    sums = add_up([rows_of(3), rows_of(4), rows_of(6, 0)], sums, 1)
    held[5], held[6][1], held[7][0], sums = barrier((held[5], held[6][1], held[7][0], sums))
    held[7].append(exchange(held[6][1], "wide", 1))
    sums = add_up([rows_of(5), rows_of(6, 1), rows_of(7, 0)], sums, 1)
    held[7][1], sums = barrier((held[7][1], sums))
    step = 8
    while step < wide_count:
        for key in range(step):
            held[key ^ step] = [exchange(part, "wide", step) for part in held[key]]
        for key in range(step, 2 * step, 2):
            sums = add_up([rows_of(k, p) for k in (key, key + 1) for p in range(len(held[k]))], sums)
        step *= 2
    slab, local, sums = barrier((slab, node_local, sums))
    ids = (slab * node_dev + local).reshape(-1, 1)
    far = [k for k in range(narrow_count) if k >= 2]
    near = [k for k in range(narrow_count) if k < 2]
    jobs = [(k, 0) for k in far]
    rounded, own, *shares = scatter_and_layer(
        place, [rows_of(7, 1)], slots, sums, matrix, jobs, 2, nodes, node_dev, 1
    )
    crossed = [exchange(share, "narrow", k) for share, (k, _) in zip(shares, jobs)]
    jobs = [(k, 0) for k in near] + [(k, 1) for k in far]
    shares = layer_more(place, rounded, own, matrix, diagonal, jobs, 2, 1)
    *crossed, upper = barrier((*crossed, shares[0]))
    crossed += [exchange(share, "narrow", k) for share, (k, _) in zip(shares[1 : len(near)], jobs[1:])]
    crossed_more = [exchange(share, "narrow", k) for share, (k, _) in zip(shares[len(near) :], jobs[len(near) :])]
    shares = layer_more(place, rounded, own, matrix, diagonal, [(k, 1) for k in near], 2, 1)
    *crossed, lower = barrier((*crossed, shares[0]))
    crossed_more += [exchange(share, "narrow", k) for share, k in zip(shares[1:], near[1:])]
    for part in crossed:
        upper = upper + part.astype(jnp.float32)
    sent = (upper * RESULT_SCALE).astype(jnp.float16)
    first = gather_far((sent, None), False)
    for part in crossed_more:
        lower = lower + part.astype(jnp.float32)
    sent = (lower * RESULT_SCALE).astype(jnp.float16)
    second = gather_far((sent, None), False)

    def look_up(keys, before, weight=1):
        blocks = [(first, second)[part][k][0].astype(jnp.float32) for k, part in keys]
        return read_back(place, ids, blocks, keys, 2, node_dev, before, weight)

    def both_parts(*keys):
        return [(k, part) for part in range(2) for k in keys]

    far4, far6 = first[4][0], first[6][0]
    first[4] = [after(far4, first[1][0], second[1][0])]
    first[2], second[2] = [after(first[2][0], far4, far6)], [after(second[2][0], far4, far6)]
    for held in (first, second):
        held[3] = [exchange(held[2][0], "wide", 1)]
        held[5] = [exchange(held[4][0], "wide", 1)]
        held[7] = [exchange(held[6][0], "wide", 1)]
    found = look_up(both_parts(0, 1, 2), None, 0)
    found = look_up(both_parts(3, 4, 6) + [(5, 0), (7, 0)], found, 0)
    second[5], second[7], found = barrier((second[5], second[7], found))
    step = 8
    while step < wide_count:
        for held in (first, second):
            for key in range(step):
                held[key ^ step] = [exchange(held[key][0], "wide", step)]
        for key in range(step, 2 * step, 4):
            found = look_up(both_parts(*range(key, key + 4)), found)
        step *= 2
    dirichlet = look_up([(5, 1), (7, 1)], found)
    potential = jnp.concatenate([upper, lower], axis=0)
    return (potential[None], dirichlet)


def solution(mesh):
    placed = (
        P(("wide", "narrow"), None),
        P(("wide", "narrow"), None),
        P(("wide", "narrow")),
        P("narrow", "wide"),
        P(None, "wide", "narrow", None),
    )
    return jax.shard_map(
        on_device,
        mesh=mesh,
        in_specs=placed,
        out_specs=(P("narrow", "wide", None), P(("wide", "narrow"), None)),
        check_vma=False,
    )
```

```python
import jax
import jax.numpy as jnp
from jax import lax
from jax.experimental import pallas as pl
from jax.experimental.pallas import tpu as pltpu
from jax.sharding import PartitionSpec as P

TRACE_SCALE = 2.0**13
RESULT_SCALE = 2.0
MIB = 2**20
ROWS = 8
EXACT = 2048


def exchange(block, axis, offset):
    count = lax.axis_size(axis)
    return lax.ppermute(block, axis, [(i, i ^ offset) for i in range(count)])


def after(value, *others):
    return lax.optimization_barrier((value, *others))[0]


def gather_far(parts, split):
    whole, pieces = parts
    held = {0: [whole]}
    held[4] = [exchange(whole, "wide", 4)]
    held[2] = [exchange(whole, "wide", 2)]
    held[1] = [exchange(whole, "wide", 1)]
    if split:
        held[6] = [exchange(pieces[0], "wide", 6), exchange(after(pieces[1], held[2][0]), "wide", 6)]
    else:
        held[6] = [exchange(whole, "wide", 6)]
    return held


def id_parts(slab, local, nodes, node_dev):
    return [slab * node_dev + local] if nodes <= EXACT else [slab, local]


def with_ids(values, parts):
    slots, images = values.shape
    per = -(-slots // images)
    extra = -(-len(parts) * per // ROWS) * ROWS
    total = jnp.pad(values, ((extra, 0), (0, 0)))
    for n, part in enumerate(parts):
        for r in range(per):
            piece = part.reshape(1, slots)[:, r * images : (r + 1) * images].astype(values.dtype)
            row = n * per + r
            total = total + jnp.pad(piece, ((row, extra + slots - row - 1), (0, images - piece.shape[1])))
    return total.astype(jnp.float16)


def ids_of(tail, slots, nodes, node_dev):
    images = tail.shape[1]
    per = -(-slots // images)

    def line(first):
        pieces = [tail[first + r : first + r + 1, : min(images, slots - r * images)] for r in range(per)]
        return pieces[0] if per == 1 else jnp.concatenate(pieces, axis=1)

    return (line(0) if nodes <= EXACT else line(0) * node_dev + line(per)).astype(jnp.int32)


def store_halves(values, out, first):
    rows, images = values.shape
    high = values.astype(jnp.bfloat16)
    out[first : first + rows, :images] = high
    out[first : first + rows, images:] = (values - high.astype(jnp.float32)).astype(jnp.bfloat16)


def cost(flops, moved, weight):
    return pl.CostEstimate(flops=int(flops * weight) + 1, bytes_accessed=int(moved * weight) + 1, transcendentals=0)


class Rows:
    def __init__(self, data, tail, first, span):
        self.data, self.tail, self.first, self.span = data, tail, first, span
        self.count = span[1] - span[0]


def row_specs(rows):
    return [pl.BlockSpec(memory_space=pltpu.VMEM)] * (2 * len(rows))


def row_args(rows):
    return [array for part in rows for array in (part.data, part.tail)]


def scatter_tile(rows, refs, both, first_node, tile, slots, nodes, node_dev):
    @pl.when(first_node == 0)
    def _():
        done = 0
        for part, data in zip(rows, refs[::2]):
            store_halves(data[part.first : part.first + part.count, :], both, done)
            done += part.count

    picks = []
    for part, tail in zip(rows, refs[1::2]):
        node = lax.broadcasted_iota(jnp.int32, (tile, part.count), 0)
        ids = ids_of(tail, slots, nodes, node_dev)[:, part.span[0] : part.span[1]] - first_node
        picks.append(jnp.where(ids == node, 1.0, 0.0).astype(jnp.bfloat16))
    total = jnp.dot(jnp.concatenate(picks, axis=1), both[...], preferred_element_type=jnp.float32)
    images = total.shape[1] // 2
    return total[:, :images] + total[:, images:]


def scatter(rows, slots, before, nodes, node_dev, weight):
    images = rows[0].data.shape[1]
    tile = 4 * node_dev
    depth = sum(part.count for part in rows)

    def body(*refs):
        out, both = refs[-2:]
        total = scatter_tile(rows, refs[: 2 * len(rows)], both, pl.program_id(0) * tile, tile, slots, nodes, node_dev)
        if before is not None:
            total = total + refs[2 * len(rows)][...]
        out[...] = total

    part = pl.BlockSpec((tile, images), lambda s: (s, 0))
    more = [] if before is None else [before]
    return pl.pallas_call(
        body,
        grid=(nodes // tile,),
        in_specs=row_specs(rows) + [part] * len(more),
        out_specs=part,
        out_shape=jax.ShapeDtypeStruct((nodes, images), jnp.float32),
        scratch_shapes=[pltpu.VMEM((depth, 2 * images), jnp.bfloat16)],
        compiler_params=pltpu.CompilerParams(vmem_limit_bytes=(14 + 2 * -(-depth // slots)) * MIB),
        cost_estimate=cost(4 * depth * nodes * images, 8 * nodes * images, weight),
        name="scatter_traces",
    )(*row_args(rows), *more)


def row_block(place_ref, job, parts):
    offset, part = job
    return (place_ref[1] ^ offset) * parts + part


def scatter_and_layer(place, rows, slots, before, matrix, jobs, parts, nodes, node_dev, weight):
    images = rows[0].data.shape[1]
    tile = 4 * node_dev
    steps = nodes // tile
    depth = sum(part.count for part in rows)
    count = len(jobs)
    height = node_dev // parts

    def body(place_ref, *refs):
        before_ref, matrix_ref = refs[2 * len(rows) : 2 * len(rows) + 2]
        rounded, own = refs[2 * len(rows) + 2 : 2 * len(rows) + 4]
        outs = refs[2 * len(rows) + 4 : -3]
        both, matrix_held, sems = refs[-3:]
        step = pl.program_id(0)
        fetches = []
        for n, job in enumerate(jobs):
            first = pl.multiple_of(row_block(place_ref, job, parts) * height, height)
            fetches.append(
                pltpu.make_async_copy(matrix_ref.at[pl.ds(first, height), :], matrix_held.at[n], sems.at[n])
            )

        @pl.when(step == 0)
        def _():
            for fetch in fetches:
                fetch.start()

        total = scatter_tile(rows, refs[: 2 * len(rows)], both, step * tile, tile, slots, nodes, node_dev)
        total = (total + before_ref[...]) * (1.0 / TRACE_SCALE)
        for slab in range(tile // node_dev):
            @pl.when(tile // node_dev * step + slab == place_ref[0])
            def _():
                own[...] = total[slab * node_dev : (slab + 1) * node_dev, :]

        rounded[pl.ds(pl.multiple_of(step * tile, tile), tile), :] = total.astype(jnp.bfloat16)

        @pl.when(step == steps - 1)
        def _():
            for n, fetch in enumerate(fetches):
                fetch.wait()
                layer = jnp.dot(matrix_held[n], rounded[...], preferred_element_type=jnp.float32)
                outs[n][...] = layer.astype(outs[n].dtype)

    one = pl.BlockSpec((height, images), lambda s, p: (0, 0))
    limit = 16 + 2 * -(-depth // slots) + (2 * count * height * nodes + 4 * nodes * images) // MIB
    return pl.pallas_call(
        body,
        grid_spec=pltpu.PrefetchScalarGridSpec(
            num_scalar_prefetch=1,
            grid=(steps,),
            in_specs=row_specs(rows)
            + [pl.BlockSpec((tile, images), lambda s, p: (s, 0)), pl.BlockSpec(memory_space=pl.ANY)],
            out_specs=[
                pl.BlockSpec((nodes, images), lambda s, p: (0, 0)),
                pl.BlockSpec((node_dev, images), lambda s, p: (0, 0)),
            ]
            + [one] * count,
            scratch_shapes=[
                pltpu.VMEM((depth, 2 * images), jnp.bfloat16),
                pltpu.VMEM((count, height, nodes), matrix.dtype),
                pltpu.SemaphoreType.DMA((count,)),
            ],
        ),
        out_shape=[
            jax.ShapeDtypeStruct((nodes, images), jnp.bfloat16),
            jax.ShapeDtypeStruct((node_dev, images), jnp.float32),
        ]
        + [jax.ShapeDtypeStruct((height, images), jnp.bfloat16)] * count,
        compiler_params=pltpu.CompilerParams(vmem_limit_bytes=limit * MIB),
        cost_estimate=cost(
            (4 * depth + 2 * count * height) * nodes * images, 8 * nodes * images, weight
        ),
        name="scatter_and_layer",
    )(place, *row_args(rows), before, matrix)


def layer_more(place, rounded, own, matrix, diagonal, jobs, parts, weight):
    node_dev, images = own.shape
    nodes = rounded.shape[0]
    count = len(jobs)
    height = node_dev // parts

    def body(place_ref, rounded_ref, own_ref, diagonal_ref, *refs):
        for n, (offset, part) in enumerate(jobs):
            layer = jnp.dot(refs[n][...], rounded_ref[...], preferred_element_type=jnp.float32)
            if offset == 0:
                here = slice(part * height, (part + 1) * height)
                layer = layer + diagonal_ref[here, :] * own_ref[here, :]
            refs[count + n][...] = layer.astype(refs[count + n].dtype)

    def spec(array):
        return pl.BlockSpec(array.shape, lambda i, p: (0, 0))

    return pl.pallas_call(
        body,
        grid_spec=pltpu.PrefetchScalarGridSpec(
            num_scalar_prefetch=1,
            grid=(1,),
            in_specs=[spec(rounded), spec(own), spec(diagonal)]
            + [pl.BlockSpec((height, nodes), lambda i, p, job=job: (row_block(p, job, parts), 0)) for job in jobs],
            out_specs=[pl.BlockSpec((height, images), lambda i, p: (0, 0))] * count,
        ),
        out_shape=[
            jax.ShapeDtypeStruct((height, images), jnp.float32 if offset == 0 else jnp.bfloat16)
            for offset, _ in jobs
        ],
        compiler_params=pltpu.CompilerParams(
            vmem_limit_bytes=(8 + (4 * nodes * images + 4 * count * height * nodes) // MIB) * MIB
        ),
        cost_estimate=cost(2 * count * height * nodes * images, 2 * nodes * images, weight),
        name="layer_more",
    )(place, rounded, own, diagonal, *[matrix] * count)


def read_back(place, ids, blocks, keys, parts, node_dev, before, weight):
    slots = ids.shape[0]
    height, images = blocks[0].shape

    def body(place_ref, ids_ref, *refs):
        out, both = refs[-2:]
        place_in = ids_ref[...] - lax.broadcasted_iota(jnp.int32, (slots, height), 1)
        picks = []
        for row, (key, part) in enumerate(keys):
            store_halves(refs[row][...], both, row * height)
            first = (place_ref[0] ^ key) * node_dev + part * height
            picks.append(jnp.where(place_in == first, 1.0, 0.0).astype(jnp.bfloat16))
        total = jnp.dot(jnp.concatenate(picks, axis=1), both[...], preferred_element_type=jnp.float32)
        total = (total[:, :images] + total[:, images:]) * (1.0 / RESULT_SCALE)
        if before is not None:
            total = total + refs[len(blocks)][...]
        out[...] = total

    more = [] if before is None else [before]
    vmem = pl.BlockSpec(memory_space=pltpu.VMEM)
    return pl.pallas_call(
        body,
        in_specs=[pl.BlockSpec(memory_space=pltpu.SMEM)] + [vmem] * (1 + len(blocks) + len(more)),
        out_shape=jax.ShapeDtypeStruct((slots, images), jnp.float32),
        scratch_shapes=[pltpu.VMEM((len(blocks) * height, 2 * images), jnp.bfloat16)],
        compiler_params=pltpu.CompilerParams(vmem_limit_bytes=(8 + 2 * len(blocks)) * MIB),
        cost_estimate=cost(4 * len(blocks) * height * slots * images, 8 * slots * images, weight),
        name="read_back",
    )(place, ids, *blocks, *more)


def on_device(trace_parts, node_slab, node_local, solid_fraction, influence):
    node_dev = solid_fraction.shape[1]
    slots, images = trace_parts.shape
    wide_count = lax.axis_size("wide")
    narrow_count = lax.axis_size("narrow")
    nodes = wide_count * node_dev
    place = jnp.stack([lax.axis_index("wide"), lax.axis_index("narrow")]).astype(jnp.int32)
    diagonal = (solid_fraction - 1.0).reshape(-1, 1)
    matrix = influence.reshape(narrow_count * node_dev, nodes)
    barrier = lax.optimization_barrier

    slab = barrier(node_slab.reshape(slots))
    parts = id_parts(slab, node_local, nodes, node_dev)
    sent = with_ids(trace_parts * TRACE_SCALE, parts)
    extra = sent.shape[0] - slots
    half = slots // 2
    held = gather_far((sent, (sent[: extra + half], sent[extra + half :])), True)

    held[3] = [exchange(held[2][0], "wide", 1)]

    def rows_of(key, part=None):
        if len(held[key]) == 1:
            data = held[key][0].astype(jnp.float32)
            return Rows(data, data, extra, (0, slots))
        tail = held[key][0].astype(jnp.float32)
        if part == 0:
            return Rows(tail, tail, extra, (0, half))
        return Rows(held[key][1].astype(jnp.float32), tail, 0, (half, slots))

    def add_up(rows, before, weight=1):
        return scatter(rows, slots, before, nodes, node_dev, weight)

    sums = add_up([rows_of(0), rows_of(1), rows_of(2)], None, 1)
    held[4] = [after(held[4][0], sums)]
    held[5] = [exchange(held[4][0], "wide", 1)]
    held[7] = [exchange(held[6][0], "wide", 1)]
    sums = add_up([rows_of(3), rows_of(4), rows_of(6, 0)], sums, 1)
    held[5], held[6][1], held[7][0], sums = barrier((held[5], held[6][1], held[7][0], sums))
    held[7].append(exchange(held[6][1], "wide", 1))
    sums = add_up([rows_of(5), rows_of(6, 1), rows_of(7, 0)], sums, 1)
    held[7][1], sums = barrier((held[7][1], sums))
    step = 8
    while step < wide_count:
        for key in range(step):
            held[key ^ step] = [exchange(part, "wide", step) for part in held[key]]
        for key in range(step, 2 * step, 2):
            sums = add_up([rows_of(k, p) for k in (key, key + 1) for p in range(len(held[k]))], sums)
        step *= 2
    slab, local, sums = barrier((slab, node_local, sums))
    ids = (slab * node_dev + local).reshape(-1, 1)
    far = [k for k in range(narrow_count) if k >= 2]
    near = [k for k in range(narrow_count) if k < 2]
    jobs = [(k, 0) for k in far]
    rounded, own, *shares = scatter_and_layer(
        place, [rows_of(7, 1)], slots, sums, matrix, jobs, 2, nodes, node_dev, 1
    )
    crossed = [exchange(share, "narrow", k) for share, (k, _) in zip(shares, jobs)]
    jobs = [(k, 0) for k in near] + [(k, 1) for k in far]
    shares = layer_more(place, rounded, own, matrix, diagonal, jobs, 2, 1)
    *crossed, upper = barrier((*crossed, shares[0]))
    crossed += [exchange(share, "narrow", k) for share, (k, _) in zip(shares[1 : len(near)], jobs[1:])]
    crossed_more = [exchange(share, "narrow", k) for share, (k, _) in zip(shares[len(near) :], jobs[len(near) :])]
    shares = layer_more(place, rounded, own, matrix, diagonal, [(k, 1) for k in near], 2, 1)
    *crossed, lower = barrier((*crossed, shares[0]))
    crossed_more += [exchange(share, "narrow", k) for share, k in zip(shares[1:], near[1:])]
    for part in crossed:
        upper = upper + part.astype(jnp.float32)
    sent = (upper * RESULT_SCALE).astype(jnp.float16)
    first = gather_far((sent, None), False)
    for part in crossed_more:
        lower = lower + part.astype(jnp.float32)
    sent = (lower * RESULT_SCALE).astype(jnp.float16)
    second = gather_far((sent, None), False)

    def look_up(keys, before, weight=1):
        blocks = [(first, second)[part][k][0].astype(jnp.float32) for k, part in keys]
        return read_back(place, ids, blocks, keys, 2, node_dev, before, weight)

    def both_parts(*keys):
        return [(k, part) for part in range(2) for k in keys]

    far4, far6 = first[4][0], first[6][0]
    first[4] = [after(far4, first[1][0], second[1][0])]
    first[2], second[2] = [after(first[2][0], far4, far6)], [after(second[2][0], far4, far6)]
    for held in (first, second):
        held[3] = [exchange(held[2][0], "wide", 1)]
        held[5] = [exchange(held[4][0], "wide", 1)]
        held[7] = [exchange(held[6][0], "wide", 1)]
    found = look_up(both_parts(0, 1, 2), None, 0)
    found = look_up(both_parts(3, 4, 6) + [(5, 0), (7, 0)], found, 0)
    second[5], second[7], found = barrier((second[5], second[7], found))
    step = 8
    while step < wide_count:
        for held in (first, second):
            for key in range(step):
                held[key ^ step] = [exchange(held[key][0], "wide", step)]
        for key in range(step, 2 * step, 4):
            found = look_up(both_parts(*range(key, key + 4)), found)
        step *= 2
    dirichlet = look_up([(5, 1), (7, 1)], found)
    potential = jnp.concatenate([upper, lower], axis=0)
    return (potential[None], dirichlet)


def solution(mesh):
    placed = (
        P(("wide", "narrow"), None),
        P(("wide", "narrow"), None),
        P(("wide", "narrow")),
        P("narrow", "wide"),
        P(None, "wide", "narrow", None),
    )
    return jax.shard_map(
        on_device,
        mesh=mesh,
        in_specs=placed,
        out_specs=(P("narrow", "wide", None), P(("wide", "narrow"), None)),
        check_vma=False,
    )
```
